512 devices in a mesh: ctx: 32 (over z, x), tp: 16 (over y, core).
Axes of the slice: x: 4, y: 8, z: 8, core: 2. Of those that a mesh axis runs over, the one named last changes fastest.
Arguments:
- x_heads: bfloat16 [4, 8192, 4096], P(None, ('ctx', 'tp')), may hold values from -6 to 6
- b_keys: bfloat16 [4, 8192, 2048], P(None, ('ctx', 'tp')), may hold values from -6 to 6
- c_queries: bfloat16 [4, 8192, 2048], P(None, ('ctx', 'tp')), may hold values from -0.005859375 to 0.005859375
- log_decay: float32 [4, 8192, 64], P(None, ('ctx', 'tp')), may hold values from -1 to 0, as said below
- level_log: float32 [4, 8192, 896], P(None, ('ctx', 'tp')), may hold values from -1 to 1
- skip_gain: float32 [64], P('tp'), may hold values from 0.1 to 1.9
Outputs:
- mixed: bfloat16 [4, 8192, 4096], P(None, ('ctx', 'tp'))
The draws below stay inside these ranges and needn't reach their ends.
Inputs may be any that keep to these rules, and one draw needn't show every extreme that they name: `log_decay`: log-decay of each position and head; negative.
All inputs are finite; a program needn't handle non-finite values.
Results may differ from the reference program's by a relative error of at most 0.0036.
Values may be sent and summed in bfloat16 or wider, within the bound.
No kernel may reach another device: no remote copies, remote signals or barrier semaphores. Data moves between devices by JAX's collectives and lax.ppermute only.
A program may use at most 128 MiB of HBM per device.

```python
import jax
import jax.numpy as jnp
from jax import lax

HEAD_COUNT = 64
HEAD_DIM = 64
STATE = 128
GROUPS = 16
LEVELS = 14
SEQUENCE_COUNT = 4
SEQUENCE_LENGTH = 8192
CTX_BITS = 5
SPAN = 256
SPAN_LEVELS = 9


def draw_log_decay(key, part):
    key = jax.random.fold_in(key, 7)
    random_key_series = jax.random.split(key, 7)
    block_total = SEQUENCE_LENGTH // SPAN
    fast_share = 0.5
    token_multiplier = jnp.exp(jax.random.uniform(random_key_series[0], (SEQUENCE_COUNT, SEQUENCE_LENGTH, HEAD_COUNT), jnp.float32, -0.69, 0.69))
    fast_heads = jax.random.bernoulli(random_key_series[1], fast_share, (SEQUENCE_COUNT, 1, HEAD_COUNT))
    slow_rate = jnp.exp(jax.random.uniform(random_key_series[2], (SEQUENCE_COUNT, 1, HEAD_COUNT), jnp.float32, jnp.log(0.02), jnp.log(0.7))) / SEQUENCE_LENGTH
    fast_rate = jnp.exp(jax.random.uniform(random_key_series[3], (SEQUENCE_COUNT, 1, HEAD_COUNT), jnp.float32, jnp.log(1.0 / 50.0), jnp.log(1.0 / 30.0)))
    baseline_rate = jnp.where(fast_heads, fast_rate, slow_rate)
    block_multiplier = jnp.exp(jax.random.uniform(random_key_series[4], (SEQUENCE_COUNT, block_total, 1, HEAD_COUNT), jnp.float32, -0.69, 0.69))
    block_multiplier = jnp.broadcast_to(block_multiplier, (SEQUENCE_COUNT, block_total, SPAN, HEAD_COUNT)).reshape(SEQUENCE_COUNT, SEQUENCE_LENGTH, HEAD_COUNT)
    spike_locations = jax.random.randint(random_key_series[5], (SEQUENCE_COUNT, 3, 1), 0, SEQUENCE_LENGTH)
    token_position = jnp.arange(SEQUENCE_LENGTH, dtype=jnp.int32)[None, None, :]
    spike_mask = jnp.any(token_position == spike_locations, axis=1)[:, :, None]
    spike_dropout = jax.random.uniform(random_key_series[6], (SEQUENCE_COUNT, SEQUENCE_LENGTH, HEAD_COUNT), jnp.float32, jnp.log(0.5), jnp.log(0.8))
    return -(baseline_rate * block_multiplier * token_multiplier) + jnp.where(spike_mask, spike_dropout, 0.0)


def shard_levels(key, extent, cuts, low, top_value):
    def one(dim, blocks):
        heights = jax.random.uniform(jax.random.fold_in(jax.random.fold_in(key, 6), dim), (blocks,), jnp.float32, low / len(cuts), top_value / len(cuts))
        return jnp.repeat(jnp.exp(heights), extent[dim] // blocks).reshape((-1,) + (1,) * (len(extent) - dim - 1))

    level = one(*cuts[0])
    for cut in cuts[1:]:
        level = level * one(*cut)
    return level


def noise(rng, extent, deviation, most, shards=(), kind=jnp.bfloat16):
    entries = deviation * jax.random.normal(rng, extent, jnp.float32)
    if shards:
        entries = entries * shard_levels(rng, extent, shards, -0.22, 0.18)
    return jnp.clip(entries, -most, most).astype(kind)


def setup_inputs(seed: int = 0) -> dict:
    splits = jax.random.split(jax.random.key(seed), 7)
    return {
        "x_heads": noise(splits[0], (SEQUENCE_COUNT, SEQUENCE_LENGTH, HEAD_COUNT * HEAD_DIM), 1.0, 6.0, ((1, 512),)),
        "b_keys": noise(splits[1], (SEQUENCE_COUNT, SEQUENCE_LENGTH, GROUPS * STATE), 1.0, 6.0, ((1, 512),)),
        "c_queries": noise(splits[2], (SEQUENCE_COUNT, SEQUENCE_LENGTH, GROUPS * STATE), (STATE * SEQUENCE_LENGTH) ** -0.5, 0.005859375, ((1, 512),)),
        "log_decay": draw_log_decay(jax.random.fold_in(splits[6], 71), 0),
        "level_log": jnp.clip(jax.random.uniform(splits[4], (SEQUENCE_COUNT, SEQUENCE_LENGTH, HEAD_COUNT * LEVELS), jnp.float32, -1.0, 1.0) * shard_levels(splits[4], (SEQUENCE_COUNT, SEQUENCE_LENGTH, HEAD_COUNT * LEVELS), ((1, 512),), -0.4, 0.0), -1.0, 1.0),
        "skip_gain": jnp.clip(1.0 + 0.18 * jax.random.normal(splits[5], (HEAD_COUNT,), jnp.float32), 0.1, 1.9),
    }


def level_matrix(length):
    token_position = jnp.arange(length, dtype=jnp.int32)
    xor_bits = jnp.bitwise_xor(token_position[:, None], token_position[None, :])
    levels_of = jnp.zeros((length, length), jnp.int32)
    for bit_power in range(length.bit_length()):
        levels_of = levels_of + (xor_bits >= (1 << bit_power)).astype(jnp.int32)
    return levels_of


def reference(x_heads, b_keys, c_queries, log_decay, level_log, skip_gain):
    per_group = HEAD_COUNT // GROUPS
    block_total = SEQUENCE_LENGTH // SPAN
    levels_of = level_matrix(SPAN)
    token_position = jnp.arange(SPAN, dtype=jnp.int32)
    causal = token_position[:, None] >= token_position[None, :]
    block_ids = jnp.arange(block_total, dtype=jnp.int32)

    def one_sequence(seq_in):
        x_seq, b_seq, c_seq, decay_seq, gate_seq = seq_in
        x_blocks = x_seq.reshape(block_total, SPAN, HEAD_COUNT, HEAD_DIM)
        b_blocks = b_seq.reshape(block_total, SPAN, GROUPS, STATE)
        c_blocks = c_seq.reshape(block_total, SPAN, GROUPS, STATE)
        cum_log = jnp.cumsum(decay_seq.reshape(block_total, SPAN, HEAD_COUNT), axis=1)
        gate_vals = jnp.exp(gate_seq.reshape(block_total, SPAN, HEAD_COUNT, LEVELS))

        def local_block(block_in):
            x_block, b_block, c_block, cum_block, gate_block = block_in
            dot_scores = jnp.einsum('tgn,sgn->gts', c_block.astype(jnp.float32), b_block.astype(jnp.float32))
            dot_heads = jnp.repeat(dot_scores, per_group, axis=0)
            cum_heads = cum_block.T
            log_gap = cum_heads[:, :, None] - cum_heads[:, None, :]
            decay_mat = jnp.where(causal, jnp.exp(jnp.where(causal, log_gap, 0.0)), 0.0)
            gate_heads = jnp.transpose(gate_block, (1, 0, 2))
            picked = jnp.zeros((HEAD_COUNT, SPAN, SPAN), jnp.float32)
            for level_id in range(SPAN_LEVELS):
                picked = picked + jnp.where(levels_of == level_id, gate_heads[:, :, level_id][:, :, None], 0.0)
            scores = (dot_heads * decay_mat * picked).astype(jnp.bfloat16)
            near_part = jnp.einsum('hts,shp->thp', scores.astype(jnp.float32), x_block.astype(jnp.float32))
            key_decay = jnp.exp(cum_block[-1:, :] - cum_block)
            b_heads = jnp.repeat(b_block, per_group, axis=1)
            keys_scaled = (b_heads.astype(jnp.float32) * key_decay[:, :, None]).astype(jnp.bfloat16)
            states = jnp.einsum('thn,thp->hnp', keys_scaled.astype(jnp.float32), x_block.astype(jnp.float32))
            return near_part, states

        near_all, states_all = lax.map(local_block, (x_blocks, b_blocks, c_blocks, cum_log, gate_vals))
        totals = cum_log[:, -1, :]
        before = jnp.cumsum(totals, axis=0) - totals

        def far_block(block_in):
            block_index, c_block, cum_block, gate_block = block_in
            c_heads = jnp.repeat(c_block, per_group, axis=1).astype(jnp.float32)
            far_part = jnp.zeros((SPAN, HEAD_COUNT, HEAD_DIM), jnp.float32)
            block_gap = before[block_index][None, :] - before - totals
            for bit_pos in range(CTX_BITS):
                member = ((block_ids >> (bit_pos + 1)) == (block_index >> (bit_pos + 1))) & (((block_ids >> bit_pos) & 1) == 0) & (((block_index >> bit_pos) & 1) == 1)
                weights = jnp.where(member[:, None], jnp.exp(jnp.where(member[:, None], block_gap, 0.0)), 0.0)
                level_state = jnp.einsum('jh,jhnp->hnp', weights, states_all, precision=lax.Precision.HIGHEST).astype(jnp.bfloat16)
                raw_part = jnp.einsum('thn,hnp->thp', c_heads, level_state.astype(jnp.float32))
                far_part = far_part + (gate_block[:, :, SPAN_LEVELS + bit_pos] * jnp.exp(cum_block))[:, :, None] * raw_part
            return far_part

        far_all = lax.map(far_block, (block_ids, c_blocks, cum_log, gate_vals))
        mixed_out = near_all + far_all + skip_gain[None, None, :, None] * x_blocks.astype(jnp.float32)
        return mixed_out.astype(jnp.bfloat16).reshape(SEQUENCE_LENGTH, HEAD_COUNT * HEAD_DIM)

    return lax.map(one_sequence, (x_heads, b_keys, c_queries, log_decay, level_log))
```

```python
import functools

import jax
import jax.numpy as jnp
from jax import lax
from jax.experimental import pallas as pl
from jax.experimental.pallas import tpu as pltpu
from jax.sharding import Mesh
from jax.sharding import PartitionSpec as P

SEQS = 4
HEADS = 64
HEAD_DIM = 64
STATE = 128
GROUPS = 16
PER_GROUP = 4
LEVELS = 14
NEAR_LEVELS = 9
CHUNK = 1024
BLOCK = 256
SUB = 64
ROWS = 72
WIDTH = PER_GROUP * HEAD_DIM
GATES = PER_GROUP * LEVELS
F32 = jnp.float32
BF16 = jnp.bfloat16
VMEM_LIMIT = 48 * 1024 * 1024


def dot(a, b):
    return jnp.dot(a, b, preferred_element_type=F32)


def dot_t(a, b):
    return lax.dot_general(a, b, (((0,), (0,)), ((), ())), preferred_element_type=F32)


def dot_nt(a, b):
    return lax.dot_general(a, b, (((1,), (1,)), ((), ())), preferred_element_type=F32)


def params():
    return pltpu.CompilerParams(vmem_limit_bytes=VMEM_LIMIT)


def pack_kernel(x_ref, b_ref, c_ref, decay_ref, level_ref, out_ref):
    gates = jnp.exp(level_ref[0])
    decay = decay_ref[0]
    high = decay.astype(BF16).astype(F32)
    low = decay - high
    for g in range(GROUPS):
        out_ref[g, 0:16, :] = x_ref[0, :, g * WIDTH : g * WIDTH + 128]
        out_ref[g, 16:32, :] = x_ref[0, :, g * WIDTH + 128 : (g + 1) * WIDTH]
        out_ref[g, 32:48, :] = b_ref[0, :, g * STATE : (g + 1) * STATE]
        out_ref[g, 48:64, :] = c_ref[0, :, g * STATE : (g + 1) * STATE]
        heads = slice(g * PER_GROUP, (g + 1) * PER_GROUP)
        piece = jnp.concatenate(
            [gates[:, g * GATES : (g + 1) * GATES], high[:, heads], low[:, heads]], axis=1
        )
        out_ref[g, 64:72, :] = jnp.concatenate([piece[0:8], piece[8:16]], axis=1).astype(BF16)


def pack(x, b, c, decay, level):
    def spec(arr):
        return pl.BlockSpec((1,) + arr.shape[1:], lambda q: (q, 0, 0))

    return pl.pallas_call(
        pack_kernel,
        grid=(SEQS,),
        in_specs=[spec(a) for a in (x, b, c, decay, level)],
        out_specs=pl.BlockSpec((GROUPS, ROWS, 128), lambda q: (q, 0, 0)),
        out_shape=jax.ShapeDtypeStruct((SEQS * GROUPS, ROWS, 128), BF16),
        compiler_params=params(),
        name="pack_messages",
    )(x, b, c, decay, level)


def load_rows(ref, first, count, start, stop):
    part = ref[pl.ds(first // 16, count // 16), start:stop, :]
    return part.reshape(count, 128)


def load_x(ref, first, count):
    return jnp.concatenate(
        [load_rows(ref, first, count, 0, 16), load_rows(ref, first, count, 16, 32)], axis=1
    )


def load_b(ref, first, count):
    return load_rows(ref, first, count, 32, 48)


def load_c(ref, first, count):
    return load_rows(ref, first, count, 48, 64)


def unpack_gates(ref, gate_ref):
    both = ref[:, 64:72, :].astype(F32)
    gate_ref[:, 0:8, :] = both[:, :, 0:64]
    gate_ref[:, 8:16, :] = both[:, :, 64:128]


def load_gates(gate_ref, first, count):
    return gate_ref[pl.ds(first // 16, count // 16)].reshape(count, 64).astype(BF16)


def spread(offset, stride):
    row = lax.broadcasted_iota(jnp.int32, (64, WIDTH), 0)
    head = lax.broadcasted_iota(jnp.int32, (64, WIDTH), 1) // HEAD_DIM
    return jnp.where(row == offset + stride * head, 1.0, 0.0).astype(BF16)


def chunk_cumsum(gate_ref, cum_ref):
    row = lax.broadcasted_iota(jnp.int32, (BLOCK, BLOCK), 0)
    col = lax.broadcasted_iota(jnp.int32, (BLOCK, BLOCK), 1)
    lower = jnp.where(row >= col, 1.0, 0.0).astype(BF16)
    to_high = spread(GATES, 1)
    to_low = spread(GATES + PER_GROUP, 1)
    offset = jnp.zeros((1, WIDTH), F32)
    for k in range(CHUNK // BLOCK):
        gates = load_gates(gate_ref, k * BLOCK, BLOCK)
        high = dot(gates, to_high).astype(BF16)
        low = dot(gates, to_low).astype(BF16)
        cum = dot(lower, high) + dot(lower, low) + offset
        cum_ref[k * BLOCK : (k + 1) * BLOCK, :] = cum
        offset = cum[BLOCK - 1 :, :]
    return offset


def split_rows(total):
    high = total.astype(BF16).astype(F32)
    middle = (total - high).astype(BF16).astype(F32)
    low = total - high - middle
    row = lax.broadcasted_iota(jnp.int32, (16, WIDTH), 0)
    rows = jnp.where(row == 0, high, jnp.where(row == 1, middle, jnp.where(row == 2, low, 0.0)))
    return rows.astype(BF16)


def message_state(ref):
    return ref[0:STATE, :].astype(F32)


def message_total(ref):
    rows = ref[STATE : STATE + 16, :].astype(F32)
    return rows[0:1] + rows[1:2] + rows[2:3]


def state_kernel(ref, out_ref, gate_ref, cum_ref):
    unpack_gates(ref, gate_ref)
    total = chunk_cumsum(gate_ref, cum_ref)
    state = jnp.zeros((STATE, WIDTH), F32)
    for k in range(CHUNK // BLOCK):
        x = load_x(ref, k * BLOCK, BLOCK).astype(F32)
        tail = jnp.exp(total - cum_ref[k * BLOCK : (k + 1) * BLOCK, :])
        state += dot_t(load_b(ref, k * BLOCK, BLOCK), (x * tail).astype(BF16))
    out_ref[0:STATE, :] = state.astype(BF16)
    out_ref[STATE : STATE + 16, :] = split_rows(total)


def chunk_state(received):
    return pl.pallas_call(
        state_kernel,
        out_shape=jax.ShapeDtypeStruct((STATE + 16, WIDTH), BF16),
        scratch_shapes=[pltpu.VMEM((64, 16, 64), F32), pltpu.VMEM((CHUNK, WIDTH), F32)],
        compiler_params=params(),
        name="chunk_state",
    )(received)


def join_kernel(bits_ref, own_ref, partner_ref, out_ref, *, bit):
    upper = bits_ref[bit] == 1
    own, own_total = message_state(own_ref), message_total(own_ref)
    partner, partner_total = message_state(partner_ref), message_total(partner_ref)
    late_total = jnp.where(upper, own_total, partner_total)
    early = jnp.where(upper, partner, own)
    late = jnp.where(upper, own, partner)
    out_ref[0:STATE, :] = (jnp.exp(late_total) * early + late).astype(BF16)
    out_ref[STATE : STATE + 16, :] = split_rows(own_total + partner_total)


def join(bits, own, partner, bit):
    return pl.pallas_call(
        functools.partial(join_kernel, bit=bit),
        in_specs=[
            pl.BlockSpec(memory_space=pltpu.SMEM),
            pl.BlockSpec(memory_space=pltpu.VMEM),
            pl.BlockSpec(memory_space=pltpu.VMEM),
        ],
        out_shape=jax.ShapeDtypeStruct(own.shape, BF16),
        compiler_params=params(),
        name="join_states",
    )(bits, own, partner)


def inner_kernel(ref, gain_ref, out_ref, grow_ref, gate_ref, cum_ref, state_ref, first_ref):
    unpack_gates(ref, gate_ref)
    chunk_cumsum(gate_ref, cum_ref)
    subs = CHUNK // SUB
    gain = gain_ref[...]

    row = lax.broadcasted_iota(jnp.int32, (SUB, WIDTH), 0)
    col = lax.broadcasted_iota(jnp.int32, (SUB, WIDTH), 1) % SUB
    differ = jnp.bitwise_xor(row, col)
    causal = row >= col
    diagonal = row == col
    head_row = lax.broadcasted_iota(jnp.int32, (PER_GROUP * SUB, WIDTH), 0) // SUB
    head_col = lax.broadcasted_iota(jnp.int32, (PER_GROUP * SUB, WIDTH), 1) // HEAD_DIM
    same_head = head_row == head_col
    spreads = [spread(level, LEVELS) for level in range(7)]

    def one_sub(i, before):
        first = i * SUB
        cum = cum_ref[pl.ds(first, SUB), :]
        last = cum[SUB - 1 :, :]
        x = load_x(ref, first, SUB)
        b = load_b(ref, first, SUB)
        c = load_c(ref, first, SUB)
        gates = load_gates(gate_ref, first, SUB)
        wide_x = x.astype(F32)
        state_ref[i] = dot_t(b, (wide_x * jnp.exp(last - cum)).astype(BF16))
        grow_ref[pl.ds(first, SUB), :] = jnp.exp(cum - before)
        first_ref[pl.ds(i, 1), :] = before
        raw = dot_nt(c, jnp.concatenate([b] * PER_GROUP, axis=0))
        cum_row = jnp.sum(jnp.where(diagonal, cum, 0.0), axis=0, keepdims=True)
        picked = dot(gates, spreads[6])
        for level in range(5, 0, -1):
            picked = jnp.where(differ < (1 << level), dot(gates, spreads[level]), picked)
        picked = jnp.where(diagonal, dot(gates, spreads[0]), picked)
        decay = jnp.exp(jnp.minimum(cum - cum_row, 0.0))
        scores = jnp.where(causal, raw * decay * picked, 0.0).astype(BF16)
        tall_x = jnp.concatenate([x] * PER_GROUP, axis=0)
        block_x = jnp.where(same_head, tall_x, jnp.zeros_like(tall_x))
        out_ref[pl.ds(first, SUB), :] = dot(scores, block_x) + gain * wide_x
        return last

    final = lax.fori_loop(0, subs, one_sub, jnp.zeros((1, WIDTH), F32))

    starts = [first_ref[i : i + 1, :] for i in range(subs)] + [final]
    states = [state_ref[i] for i in range(subs)]
    size = 1
    for bit in range(4):
        to_lanes = spread(7 + bit, LEVELS)
        for group in range(1, subs // size, 2):
            lower = states[group - 1].astype(BF16)
            for part in range(size):
                i = group * size + part
                rows = slice(i * SUB, (i + 1) * SUB)
                weight = dot(load_gates(gate_ref, i * SUB, SUB), to_lanes) * grow_ref[rows, :]
                if part:
                    weight = weight * jnp.exp(starts[i] - starts[group * size])
                out_ref[rows, :] += weight * dot(load_c(ref, i * SUB, SUB), lower)
        states = [
            states[g] * jnp.exp(starts[(g + 2) * size] - starts[(g + 1) * size]) + states[g + 1]
            for g in range(0, subs // size, 2)
        ]
        size *= 2
    for i in range(1, subs):
        rows = slice(i * SUB, (i + 1) * SUB)
        grow_ref[rows, :] = grow_ref[rows, :] * jnp.exp(starts[i])


def inner_part(received, gain):
    wide = jax.ShapeDtypeStruct((CHUNK, WIDTH), F32)
    return pl.pallas_call(
        inner_kernel,
        out_shape=(wide, wide),
        scratch_shapes=[
            pltpu.VMEM((64, 16, 64), F32),
            pltpu.VMEM((CHUNK, WIDTH), F32),
            pltpu.VMEM((CHUNK // SUB, STATE, WIDTH), F32),
            pltpu.VMEM((CHUNK // SUB, WIDTH), F32),
        ],
        compiler_params=params(),
        cost_estimate=pl.CostEstimate(
            flops=2 * CHUNK * WIDTH * 2048, bytes_accessed=4 * 1024 * 1024, transcendentals=10**6
        ),
        name="inner_part",
    )(received, gain)


def outer_kernel(bits_ref, ref, inner_ref, grow_ref, m0_ref, m1_ref, m2_ref, out_ref):
    both = ref[:, 64:72, :].astype(F32)
    gates = jnp.concatenate([both[:, :, 0:64], both[:, :, 64:128]], axis=1)
    gates = gates.reshape(BLOCK, 64).astype(BF16)
    c = load_rows(ref, 0, BLOCK, 48, 64)
    prefix = jnp.zeros((1, WIDTH), F32)
    total = jnp.zeros((BLOCK, WIDTH), F32)
    for bit, message in enumerate((m0_ref, m1_ref, m2_ref)):
        upper = bits_ref[bit] == 1
        level_state = jnp.where(upper, jnp.exp(prefix) * message_state(message), 0.0).astype(BF16)
        prefix = prefix + jnp.where(upper, message_total(message), 0.0)
        total += dot(gates, spread(11 + bit, LEVELS)) * dot(c, level_state)
    mixed = inner_ref[...] + grow_ref[...] * total
    out_ref[...] = mixed.astype(BF16).reshape(BLOCK // 16, 16, WIDTH)


def outer_part(bits, received, inner, grow, messages):
    steps = CHUNK // BLOCK
    wide = pl.BlockSpec((BLOCK, WIDTH), lambda k: (k, 0))
    state = pl.BlockSpec((STATE + 16, WIDTH), lambda k: (0, 0))
    return pl.pallas_call(
        outer_kernel,
        grid=(steps,),
        in_specs=[
            pl.BlockSpec(memory_space=pltpu.SMEM),
            pl.BlockSpec((64 // steps, ROWS, 128), lambda k: (k, 0, 0)),
            wide,
            wide,
            state,
            state,
            state,
        ],
        out_specs=pl.BlockSpec((64 // steps, 16, WIDTH), lambda k: (k, 0, 0)),
        out_shape=jax.ShapeDtypeStruct((64, 16, WIDTH), BF16),
        compiler_params=params(),
        name="outer_part",
    )(bits, received, inner, grow, *messages)


def unpack_kernel(ref, out_ref):
    for g in range(GROUPS):
        out_ref[0, :, g * WIDTH : (g + 1) * WIDTH] = ref[g]


def unpack(received):
    return pl.pallas_call(
        unpack_kernel,
        grid=(SEQS,),
        in_specs=[pl.BlockSpec((GROUPS, 16, WIDTH), lambda q: (q, 0, 0))],
        out_specs=pl.BlockSpec((1, 16, HEADS * HEAD_DIM), lambda q: (q, 0, 0)),
        out_shape=jax.ShapeDtypeStruct((SEQS, 16, HEADS * HEAD_DIM), BF16),
        compiler_params=params(),
        name="unpack_outputs",
    )(received)


def per_device(x_heads, b_keys, c_queries, log_decay, level_log, skip_gain):
    near_axes = ("block", "tp")
    packed = pack(x_heads, b_keys, c_queries, log_decay, level_log)
    received = lax.all_to_all(packed, near_axes, 0, 0, tiled=True)
    gain = jnp.repeat(skip_gain, HEAD_DIM)[None, :]
    chunk = lax.axis_index("chunk")
    bits = jnp.stack([(chunk >> bit) & 1 for bit in range(3)]).astype(jnp.int32)
    own = chunk_state(received)
    inner, grow = inner_part(received, gain)
    messages = []
    for bit in range(3):
        pairs = [(source, source ^ (1 << bit)) for source in range(8)]
        partner = lax.ppermute(own, "chunk", pairs)
        messages.append(partner)
        if bit < 2:
            own = join(bits, own, partner, bit)
    mixed = outer_part(bits, received, inner, grow, messages)
    return unpack(lax.all_to_all(mixed, near_axes, 0, 0, tiled=True))


def solution(mesh):
    cut = Mesh(mesh.devices.reshape(8, 4, 16), ("chunk", "block", "tp"))
    split = P(None, ("chunk", "block", "tp"), None)
    return jax.shard_map(
        per_device,
        mesh=cut,
        in_specs=(split, split, split, split, split, P("tp")),
        out_specs=split,
        check_vma=False,
    )
```

```python
import jax
import jax.numpy as jnp
from jax import lax
from jax.experimental import pallas as pl
from jax.experimental.pallas import tpu as pltpu
from jax.sharding import Mesh
from jax.sharding import PartitionSpec as P

SEQS = 4
HEADS = 64
HEAD_DIM = 64
STATE = 128
GROUPS = 16
PER_GROUP = 4
LEVELS = 14
NEAR_LEVELS = 9
CHUNK = 1024
BLOCK = 256
SUB = 64
ROWS = 72
WIDTH = PER_GROUP * HEAD_DIM
GATES = PER_GROUP * LEVELS
F32 = jnp.float32
BF16 = jnp.bfloat16
VMEM_LIMIT = 48 * 1024 * 1024


def dot(a, b):
    return jnp.dot(a, b, preferred_element_type=F32)


def dot_t(a, b):
    return lax.dot_general(a, b, (((0,), (0,)), ((), ())), preferred_element_type=F32)


def dot_nt(a, b):
    return lax.dot_general(a, b, (((1,), (1,)), ((), ())), preferred_element_type=F32)


def params():
    return pltpu.CompilerParams(vmem_limit_bytes=VMEM_LIMIT)


def pack_kernel(x_ref, b_ref, c_ref, decay_ref, level_ref, out_ref):
    gates = jnp.exp(level_ref[0])
    decay = decay_ref[0]
    high = decay.astype(BF16).astype(F32)
    low = decay - high
    for g in range(GROUPS):
        out_ref[g, 0:16, :] = x_ref[0, :, g * WIDTH : g * WIDTH + 128]
        out_ref[g, 16:32, :] = x_ref[0, :, g * WIDTH + 128 : (g + 1) * WIDTH]
        out_ref[g, 32:48, :] = b_ref[0, :, g * STATE : (g + 1) * STATE]
        out_ref[g, 48:64, :] = c_ref[0, :, g * STATE : (g + 1) * STATE]
        heads = slice(g * PER_GROUP, (g + 1) * PER_GROUP)
        piece = jnp.concatenate(
            [gates[:, g * GATES : (g + 1) * GATES], high[:, heads], low[:, heads]], axis=1
        )
        out_ref[g, 64:72, :] = jnp.concatenate([piece[0:8], piece[8:16]], axis=1).astype(BF16)


def pack(x, b, c, decay, level):
    def spec(arr):
        return pl.BlockSpec((1,) + arr.shape[1:], lambda q: (q, 0, 0))

    return pl.pallas_call(
        pack_kernel,
        grid=(SEQS,),
        in_specs=[spec(a) for a in (x, b, c, decay, level)],
        out_specs=pl.BlockSpec((GROUPS, ROWS, 128), lambda q: (q, 0, 0)),
        out_shape=jax.ShapeDtypeStruct((SEQS * GROUPS, ROWS, 128), BF16),
        name="pack_messages",
    )(x, b, c, decay, level)


def load_rows(ref, first, count, start, stop):
    part = ref[pl.ds(first // 16, count // 16), start:stop, :]
    return part.reshape(count, 128)


def load_x(ref, first, count):
    return jnp.concatenate(
        [load_rows(ref, first, count, 0, 16), load_rows(ref, first, count, 16, 32)], axis=1
    )


def load_b(ref, first, count):
    return load_rows(ref, first, count, 32, 48)


def load_c(ref, first, count):
    return load_rows(ref, first, count, 48, 64)


def unpack_gates(ref, gate_ref):
    both = ref[:, 64:72, :].astype(F32)
    gate_ref[:, 0:8, :] = both[:, :, 0:64]
    gate_ref[:, 8:16, :] = both[:, :, 64:128]


def load_gates(gate_ref, first, count):
    return gate_ref[pl.ds(first // 16, count // 16)].reshape(count, 64).astype(BF16)


def spread(offset, stride):
    row = lax.broadcasted_iota(jnp.int32, (64, WIDTH), 0)
    head = lax.broadcasted_iota(jnp.int32, (64, WIDTH), 1) // HEAD_DIM
    return jnp.where(row == offset + stride * head, 1.0, 0.0).astype(BF16)


def chunk_cumsum(gate_ref, cum_ref):
    row = lax.broadcasted_iota(jnp.int32, (BLOCK, BLOCK), 0)
    col = lax.broadcasted_iota(jnp.int32, (BLOCK, BLOCK), 1)
    lower = jnp.where(row >= col, 1.0, 0.0).astype(BF16)
    to_high = spread(GATES, 1)
    to_low = spread(GATES + PER_GROUP, 1)
    offset = jnp.zeros((1, WIDTH), F32)
    for k in range(CHUNK // BLOCK):
        gates = load_gates(gate_ref, k * BLOCK, BLOCK)
        high = dot(gates, to_high).astype(BF16)
        low = dot(gates, to_low).astype(BF16)
        cum = dot(lower, high) + dot(lower, low) + offset
        cum_ref[k * BLOCK : (k + 1) * BLOCK, :] = cum
        offset = cum[BLOCK - 1 :, :]
    return offset


def split_rows(total):
    high = total.astype(BF16).astype(F32)
    middle = (total - high).astype(BF16).astype(F32)
    low = total - high - middle
    row = lax.broadcasted_iota(jnp.int32, (16, WIDTH), 0)
    rows = jnp.where(row == 0, high, jnp.where(row == 1, middle, jnp.where(row == 2, low, 0.0)))
    return rows.astype(BF16)


def message_state(ref):
    return ref[0:STATE, :].astype(F32)


def message_total(ref):
    rows = ref[STATE : STATE + 16, :].astype(F32)
    return rows[0:1] + rows[1:2] + rows[2:3]


def state_kernel(ref, out_ref, gate_ref, cum_ref):
    unpack_gates(ref, gate_ref)
    total = chunk_cumsum(gate_ref, cum_ref)
    state = jnp.zeros((STATE, WIDTH), F32)
    for k in range(CHUNK // BLOCK):
        x = load_x(ref, k * BLOCK, BLOCK).astype(F32)
        tail = jnp.exp(total - cum_ref[k * BLOCK : (k + 1) * BLOCK, :])
        state += dot_t(load_b(ref, k * BLOCK, BLOCK), (x * tail).astype(BF16))
    out_ref[0:STATE, :] = state.astype(BF16)
    out_ref[STATE : STATE + 16, :] = split_rows(total)


def chunk_state(received):
    return pl.pallas_call(
        state_kernel,
        out_shape=jax.ShapeDtypeStruct((STATE + 16, WIDTH), BF16),
        scratch_shapes=[pltpu.VMEM((64, 16, 64), F32), pltpu.VMEM((CHUNK, WIDTH), F32)],
        compiler_params=params(),
        name="chunk_state",
    )(received)


def join_kernel(place_ref, own_ref, partner_ref, near_ref, out_ref):
    upper = place_ref[0] % 2 == 1
    own, own_total = message_state(own_ref), message_total(own_ref)
    partner, partner_total = message_state(partner_ref), message_total(partner_ref)
    late_total = jnp.where(upper, own_total, partner_total)
    early = jnp.where(upper, partner, own)
    late = jnp.where(upper, own, partner)
    out_ref[0:STATE, :] = (jnp.exp(late_total) * early + late).astype(BF16)
    out_ref[STATE : STATE + 16, :] = split_rows(own_total + partner_total)


def join(place, own, partner, near):
    return pl.pallas_call(
        join_kernel,
        in_specs=[
            pl.BlockSpec(memory_space=pltpu.SMEM),
            pl.BlockSpec(memory_space=pltpu.VMEM),
            pl.BlockSpec(memory_space=pltpu.VMEM),
            pl.BlockSpec(memory_space=pl.ANY),
        ],
        out_shape=jax.ShapeDtypeStruct(own.shape, BF16),
        compiler_params=params(),
        name="join_states",
    )(place, own, partner, near)


def near_kernel(ref, gain_ref, own_ref, out_ref, gate_ref, cum_ref):
    unpack_gates(ref, gate_ref)
    chunk_cumsum(gate_ref, cum_ref)
    gain = gain_ref[...]
    row = lax.broadcasted_iota(jnp.int32, (SUB, WIDTH), 0)
    col = lax.broadcasted_iota(jnp.int32, (SUB, WIDTH), 1) % SUB
    differ = jnp.bitwise_xor(row, col)
    causal = row >= col
    diagonal = row == col
    head_row = lax.broadcasted_iota(jnp.int32, (PER_GROUP * SUB, WIDTH), 0) // SUB
    head_col = lax.broadcasted_iota(jnp.int32, (PER_GROUP * SUB, WIDTH), 1) // HEAD_DIM
    same_head = head_row == head_col
    spreads = [spread(level, LEVELS) for level in range(7)]

    @pl.loop(0, CHUNK // SUB)
    def _(i):
        first = i * SUB
        cum = cum_ref[pl.ds(first, SUB), :]
        x = load_x(ref, first, SUB)
        b = load_b(ref, first, SUB)
        c = load_c(ref, first, SUB)
        gates = load_gates(gate_ref, first, SUB)
        raw = dot_nt(c, jnp.concatenate([b] * PER_GROUP, axis=0))
        cum_row = jnp.sum(jnp.where(diagonal, cum, 0.0), axis=0, keepdims=True)
        picked = dot(gates, spreads[6])
        for level in range(5, 0, -1):
            picked = jnp.where(differ < (1 << level), dot(gates, spreads[level]), picked)
        picked = jnp.where(diagonal, dot(gates, spreads[0]), picked)
        decay = jnp.exp(jnp.minimum(cum - cum_row, 0.0))
        scores = jnp.where(causal, raw * decay * picked, 0.0).astype(BF16)
        tall_x = jnp.concatenate([x] * PER_GROUP, axis=0)
        block_x = jnp.where(same_head, tall_x, jnp.zeros_like(tall_x))
        out_ref[pl.ds(first, SUB), :] = dot(scores, block_x) + gain * x.astype(F32)


def near_part(received, gain, own):
    return pl.pallas_call(
        near_kernel,
        in_specs=[
            pl.BlockSpec(memory_space=pltpu.VMEM),
            pl.BlockSpec(memory_space=pltpu.VMEM),
            pl.BlockSpec(memory_space=pl.ANY),
        ],
        out_shape=jax.ShapeDtypeStruct((CHUNK, WIDTH), F32),
        scratch_shapes=[pltpu.VMEM((64, 16, 64), F32), pltpu.VMEM((CHUNK, WIDTH), F32)],
        compiler_params=params(),
        cost_estimate=pl.CostEstimate(
            flops=4 * 10**9, bytes_accessed=4 * 1024 * 1024, transcendentals=10**6
        ),
        name="near_part",
    )(received, gain, own)


def levels_kernel(ref, near_ref, own_ref, out_ref, grow_ref, gate_ref, cum_ref, state_ref):
    unpack_gates(ref, gate_ref)
    final = chunk_cumsum(gate_ref, cum_ref)
    subs = CHUNK // SUB
    starts = [jnp.zeros((1, WIDTH), F32)]
    starts += [cum_ref[i * SUB - 1 : i * SUB, :] for i in range(1, subs)] + [final]
    for i in range(subs):
        rows = slice(i * SUB, (i + 1) * SUB)
        x = load_x(ref, i * SUB, SUB).astype(F32)
        cum = cum_ref[rows, :]
        tail = jnp.exp(starts[i + 1] - cum)
        state_ref[i] = dot_t(load_b(ref, i * SUB, SUB), (x * tail).astype(BF16))
        grow_ref[rows, :] = jnp.exp(cum - starts[i])
        out_ref[rows, :] = near_ref[rows, :]

    states = [state_ref[i] for i in range(subs)]
    size = 1
    for bit in range(4):
        to_lanes = spread(7 + bit, LEVELS)
        for group in range(1, subs // size, 2):
            lower = states[group - 1].astype(BF16)
            for part in range(size):
                i = group * size + part
                rows = slice(i * SUB, (i + 1) * SUB)
                weight = dot(load_gates(gate_ref, i * SUB, SUB), to_lanes) * grow_ref[rows, :]
                if part:
                    weight = weight * jnp.exp(starts[i] - starts[group * size])
                out_ref[rows, :] += weight * dot(load_c(ref, i * SUB, SUB), lower)
        states = [
            states[g] * jnp.exp(starts[(g + 2) * size] - starts[(g + 1) * size]) + states[g + 1]
            for g in range(0, subs // size, 2)
        ]
        size *= 2
    for i in range(1, subs):
        rows = slice(i * SUB, (i + 1) * SUB)
        grow_ref[rows, :] = grow_ref[rows, :] * jnp.exp(starts[i])


def levels_part(received, near, own):
    wide = jax.ShapeDtypeStruct((CHUNK, WIDTH), F32)
    return pl.pallas_call(
        levels_kernel,
        in_specs=[
            pl.BlockSpec(memory_space=pltpu.VMEM),
            pl.BlockSpec(memory_space=pltpu.VMEM),
            pl.BlockSpec(memory_space=pl.ANY),
        ],
        out_shape=(wide, wide),
        scratch_shapes=[
            pltpu.VMEM((64, 16, 64), F32),
            pltpu.VMEM((CHUNK, WIDTH), F32),
            pltpu.VMEM((CHUNK // SUB, STATE, WIDTH), F32),
        ],
        compiler_params=params(),
        cost_estimate=pl.CostEstimate(
            flops=4 * 10**9, bytes_accessed=4 * 1024 * 1024, transcendentals=10**6
        ),
        name="levels_part",
    )(received, near, own)


def outer_kernel(
    place_ref, ref, inner_ref, grow_ref, pair_ref, one_ref, two_ref, three_ref, out_ref, level_ref
):
    @pl.when(pl.program_id(0) == 0)
    def _():
        place = place_ref[0]
        in_half, odd, high = place % 2 == 1, place // 2 % 2 == 1, place // 4 == 1
        level_ref[0] = jnp.where(in_half, pair_ref[0:STATE, :].astype(F32), 0.0).astype(BF16)
        prefix = jnp.where(in_half, message_total(pair_ref), 0.0)
        near_state, near_total = message_state(one_ref), message_total(one_ref)
        level_ref[1] = jnp.where(odd, jnp.exp(prefix) * near_state, 0.0).astype(BF16)
        prefix = prefix + jnp.where(odd, near_total, 0.0)
        late = jnp.where(odd, message_state(two_ref), near_state)
        late_total = jnp.where(odd, message_total(two_ref), near_total)
        early = jnp.where(odd, message_state(three_ref), message_state(two_ref))
        joined = jnp.exp(late_total) * early + late
        level_ref[2] = jnp.where(high, jnp.exp(prefix) * joined, 0.0).astype(BF16)

    both = ref[:, 64:72, :].astype(F32)
    gates = jnp.concatenate([both[:, :, 0:64], both[:, :, 64:128]], axis=1)
    gates = gates.reshape(BLOCK, 64).astype(BF16)
    c = load_rows(ref, 0, BLOCK, 48, 64)
    total = jnp.zeros((BLOCK, WIDTH), F32)
    for bit in range(3):
        total += dot(gates, spread(11 + bit, LEVELS)) * dot(c, level_ref[bit])
    mixed = inner_ref[...] + grow_ref[...] * total
    out_ref[...] = mixed.astype(BF16).reshape(BLOCK // 16, 16, WIDTH)


def outer_part(place, received, inner, grow, messages):
    steps = CHUNK // BLOCK
    wide = pl.BlockSpec((BLOCK, WIDTH), lambda k: (k, 0))
    state = pl.BlockSpec((STATE + 16, WIDTH), lambda k: (0, 0))
    return pl.pallas_call(
        outer_kernel,
        grid=(steps,),
        in_specs=[
            pl.BlockSpec(memory_space=pltpu.SMEM),
            pl.BlockSpec((64 // steps, ROWS, 128), lambda k: (k, 0, 0)),
            wide,
            wide,
            state,
            state,
            state,
            state,
        ],
        out_specs=pl.BlockSpec((64 // steps, 16, WIDTH), lambda k: (k, 0, 0)),
        out_shape=jax.ShapeDtypeStruct((64, 16, WIDTH), BF16),
        scratch_shapes=[pltpu.VMEM((3, STATE, WIDTH), BF16)],
        compiler_params=params(),
        name="outer_part",
    )(place, received, inner, grow, *messages)


def unpack_kernel(ref, out_ref):
    for g in range(GROUPS):
        out_ref[0, :, g * WIDTH : (g + 1) * WIDTH] = ref[g]


def unpack(received):
    return pl.pallas_call(
        unpack_kernel,
        grid=(SEQS,),
        in_specs=[pl.BlockSpec((GROUPS, 16, WIDTH), lambda q: (q, 0, 0))],
        out_specs=pl.BlockSpec((1, 16, HEADS * HEAD_DIM), lambda q: (q, 0, 0)),
        out_shape=jax.ShapeDtypeStruct((SEQS, 16, HEADS * HEAD_DIM), BF16),
        compiler_params=params(),
        name="unpack_outputs",
    )(received)


def per_device(x_heads, b_keys, c_queries, log_decay, level_log, skip_gain):
    near_axes = ("block", "tp")
    packed = pack(x_heads, b_keys, c_queries, log_decay, level_log)
    received = lax.all_to_all(packed, near_axes, 0, 0, tiled=True)
    gain = jnp.repeat(skip_gain, HEAD_DIM)[None, :]
    place = lax.axis_index("chunk").astype(jnp.int32)[None]
    own = chunk_state(received)
    pair = lax.ppermute(own, "chunk", [(source, source ^ 1) for source in range(8)])
    near = near_part(received, gain, own)
    own = join(place, own, pair, near)
    shifted = [
        lax.ppermute(own, "chunk", [(source, source + 2 * z) for source in range(8 - 2 * z)])
        for z in (1, 2, 3)
    ]
    inner, grow = levels_part(received, near, own)
    mixed = outer_part(place, received, inner, grow, [pair] + shifted)
    return unpack(lax.all_to_all(mixed, near_axes, 0, 0, tiled=True))


def solution(mesh):
    cut = Mesh(mesh.devices.reshape(8, 4, 16), ("chunk", "block", "tp"))
    split = P(None, ("chunk", "block", "tp"), None)
    return jax.shard_map(
        per_device,
        mesh=cut,
        in_specs=(split, split, split, split, split, P("tp")),
        out_specs=split,
        check_vma=False,
    )
```

```python
import jax
import jax.numpy as jnp
from jax import lax
from jax.experimental import pallas as pl
from jax.experimental.pallas import tpu as pltpu
from jax.sharding import Mesh
from jax.sharding import PartitionSpec as P

SEQS = 4
HEADS = 64
HEAD_DIM = 64
STATE = 128
GROUPS = 16
PER_GROUP = 4
LEVELS = 14
NEAR_LEVELS = 9
CHUNK = 1024
BLOCK = 256
SUB = 64
ROWS = 72
WIDTH = PER_GROUP * HEAD_DIM
GATES = PER_GROUP * LEVELS
CODE = 64.0
F32 = jnp.float32
BF16 = jnp.bfloat16
VMEM_LIMIT = 48 * 1024 * 1024


def dot(a, b):
    return jnp.dot(a, b, preferred_element_type=F32)


def dot_t(a, b):
    return lax.dot_general(a, b, (((0,), (0,)), ((), ())), preferred_element_type=F32)


def dot_nt(a, b):
    return lax.dot_general(a, b, (((1,), (1,)), ((), ())), preferred_element_type=F32)


def params():
    return pltpu.CompilerParams(vmem_limit_bytes=VMEM_LIMIT)


def sequence_at(block, place):
    return jnp.bitwise_xor(block, 2 * (place % 2))


def pack_kernel(place_ref, *refs):
    sources, out_ref = refs[:5], refs[5]
    x_ref, b_ref, c_ref, decay_ref, level_ref = held = refs[6:11]
    packed_ref, sems, out_sems = refs[11:]
    copies = [
        [
            pltpu.make_async_copy(
                source.at[sequence_at(k, place_ref[0])], slot.at[k], sems.at[i, k]
            )
            for i, (source, slot) in enumerate(zip(sources, held))
        ]
        for k in range(SEQS)
    ]
    for group in copies:
        for copy in group:
            copy.start()
    sends = []
    for k, group in enumerate(copies):
        for copy in group:
            copy.wait()
        gates = jnp.exp(CODE * level_ref[k])
        decay = decay_ref[k]
        high = decay.astype(BF16).astype(F32)
        low = decay - high
        for g in range(GROUPS):
            at = k * GROUPS + g
            packed_ref[at, 0:16, :] = x_ref[k, :, g * WIDTH : g * WIDTH + 128]
            packed_ref[at, 16:32, :] = x_ref[k, :, g * WIDTH + 128 : (g + 1) * WIDTH]
            packed_ref[at, 32:48, :] = b_ref[k, :, g * STATE : (g + 1) * STATE]
            packed_ref[at, 48:64, :] = c_ref[k, :, g * STATE : (g + 1) * STATE]
            heads = slice(g * PER_GROUP, (g + 1) * PER_GROUP)
            piece = jnp.concatenate(
                [gates[:, g * GATES : (g + 1) * GATES], high[:, heads], low[:, heads]], axis=1
            )
            packed_ref[at, 64:72, :] = jnp.concatenate([piece[0:8], piece[8:16]], axis=1).astype(BF16)
        part = pl.ds(k * GROUPS, GROUPS)
        sends.append(
            pltpu.make_async_copy(packed_ref.at[part], out_ref.at[part], out_sems.at[k])
        )
        sends[-1].start()
    for copy in sends:
        copy.wait()


def pack(place, *arrays):
    shape = (SEQS * GROUPS, ROWS, 128)
    return pl.pallas_call(
        pack_kernel,
        in_specs=[pl.BlockSpec(memory_space=pltpu.SMEM)]
        + [pl.BlockSpec(memory_space=pltpu.HBM)] * len(arrays),
        out_specs=pl.BlockSpec(memory_space=pltpu.HBM),
        out_shape=jax.ShapeDtypeStruct(shape, BF16),
        scratch_shapes=[pltpu.VMEM(a.shape, a.dtype) for a in arrays]
        + [
            pltpu.VMEM(shape, BF16),
            pltpu.SemaphoreType.DMA((len(arrays), SEQS)),
            pltpu.SemaphoreType.DMA((SEQS,)),
        ],
        name="pack_messages",
    )(place, *arrays)


def load_rows(ref, first, count, start, stop):
    part = ref[pl.ds(first // 16, count // 16), start:stop, :]
    return part.reshape(count, 128)


def load_x(ref, first, count):
    return jnp.concatenate(
        [load_rows(ref, first, count, 0, 16), load_rows(ref, first, count, 16, 32)], axis=1
    )


def load_b(ref, first, count):
    return load_rows(ref, first, count, 32, 48)


def load_c(ref, first, count):
    return load_rows(ref, first, count, 48, 64)


def halves_wide(value):
    high = value.astype(BF16)
    return high, value - high.astype(F32)


def halves(value):
    high = value.astype(BF16)
    return high, (value - high.astype(F32)).astype(BF16)


def spread(rows, offset, stride):
    row = lax.broadcasted_iota(jnp.int32, (rows, WIDTH), 0) % 64
    head = lax.broadcasted_iota(jnp.int32, (rows, WIDTH), 1) // HEAD_DIM
    return jnp.where(row == offset + stride * head, 1.0, 0.0).astype(BF16)


def chunk_cumsum(ref, wide_ref, cum_ref):
    both = ref[:, 64:72, :].astype(F32)
    wide_ref[:, 0:8, :] = both[:, :, 0:64]
    wide_ref[:, 8:16, :] = both[:, :, 64:128]
    row = lax.broadcasted_iota(jnp.int32, (BLOCK, BLOCK), 0)
    col = lax.broadcasted_iota(jnp.int32, (BLOCK, BLOCK), 1)
    lower = jnp.where(row >= col, 1.0, 0.0).astype(BF16)
    lane = lax.broadcasted_iota(jnp.int32, (64, WIDTH), 0)
    head = lax.broadcasted_iota(jnp.int32, (64, WIDTH), 1) // HEAD_DIM
    wanted = (lane >= GATES) & (lane % PER_GROUP == head)
    widen = jnp.where(wanted, 1.0, 0.0).astype(BF16)
    widen = jnp.concatenate([widen] * 3, axis=0)
    offset = jnp.zeros((1, WIDTH), F32)
    for k in range(CHUNK // BLOCK):
        values = wide_ref[k * 16 : (k + 1) * 16].reshape(BLOCK, 64).astype(BF16)
        sums = dot(lower, values)
        high, rest = halves_wide(sums)
        middle, rest = halves_wide(rest)
        parts = jnp.concatenate([high, middle, rest.astype(BF16)], axis=1)
        cum = dot(parts, widen) + offset
        cum_ref[k * BLOCK : (k + 1) * BLOCK, :] = cum
        offset = cum[BLOCK - 1 :, :]
    return offset


def decode_gates(ref, wide_ref, gate_ref):
    both = ref[:, 64:72, :].astype(F32)
    lane = lax.broadcasted_iota(jnp.int32, both.shape, 2) % 64
    gates = jnp.exp(jnp.log(jnp.where(lane < GATES, both, 1.0)) * (1.0 / CODE))
    wide_ref[:, 0:8, :] = gates[:, :, 0:64]
    wide_ref[:, 8:16, :] = gates[:, :, 64:128]
    high, low = halves(wide_ref[...].reshape(CHUNK, 64))
    gate_ref[...] = jnp.concatenate([high, low], axis=1)


def split_rows(total):
    high = total.astype(BF16).astype(F32)
    middle = (total - high).astype(BF16).astype(F32)
    low = total - high - middle
    row = lax.broadcasted_iota(jnp.int32, (16, WIDTH), 0)
    rows = jnp.where(row == 0, high, jnp.where(row == 1, middle, jnp.where(row == 2, low, 0.0)))
    return rows.astype(BF16)


def message_state(ref):
    return ref[0:STATE, :].astype(F32)


def message_total(ref):
    rows = ref[STATE : STATE + 16, :].astype(F32)
    return rows[0:1] + rows[1:2] + rows[2:3]


def state_kernel(ref, out_ref, cum_ref, wide_ref):
    total = chunk_cumsum(ref, wide_ref, cum_ref)
    state = jnp.zeros((STATE, WIDTH), F32)
    for k in range(CHUNK // BLOCK):
        tail = jnp.exp(total - cum_ref[k * BLOCK : (k + 1) * BLOCK, :])
        high, low = halves(load_x(ref, k * BLOCK, BLOCK).astype(F32) * tail)
        b = load_b(ref, k * BLOCK, BLOCK)
        both = dot_t(b, jnp.concatenate([high, low], axis=1))
        state += both[:, :WIDTH] + both[:, WIDTH:]
    out_ref[0:STATE, :] = state.astype(BF16)
    out_ref[STATE : STATE + 16, :] = split_rows(total)


def chunk_state(received):
    return pl.pallas_call(
        state_kernel,
        out_shape=(
            jax.ShapeDtypeStruct((STATE + 16, WIDTH), BF16),
            jax.ShapeDtypeStruct((CHUNK, WIDTH), F32),
        ),
        scratch_shapes=[pltpu.VMEM((64, 16, 64), F32)],
        compiler_params=params(),
        name="chunk_state",
    )(received)


def join_kernel(place_ref, own_ref, partner_ref, near_ref, out_ref):
    upper = place_ref[0] % 2 == 1
    own, own_total = message_state(own_ref), message_total(own_ref)
    partner, partner_total = message_state(partner_ref), message_total(partner_ref)
    late_total = jnp.where(upper, own_total, partner_total)
    early = jnp.where(upper, partner, own)
    late = jnp.where(upper, own, partner)
    out_ref[0:STATE, :] = (jnp.exp(late_total) * early + late).astype(BF16)
    out_ref[STATE : STATE + 16, :] = split_rows(own_total + partner_total)


def join(place, own, partner, near):
    return pl.pallas_call(
        join_kernel,
        in_specs=[
            pl.BlockSpec(memory_space=pltpu.SMEM),
            pl.BlockSpec(memory_space=pltpu.VMEM),
            pl.BlockSpec(memory_space=pltpu.VMEM),
            pl.BlockSpec(memory_space=pl.ANY),
        ],
        out_shape=jax.ShapeDtypeStruct(own.shape, BF16),
        compiler_params=params(),
        name="join_states",
    )(place, own, partner, near)


def near_kernel(ref, cum_ref, gain_ref, out_ref, gate_ref, wide_ref):
    decode_gates(ref, wide_ref, gate_ref)
    gain = gain_ref[...]
    row = lax.broadcasted_iota(jnp.int32, (SUB, WIDTH), 0)
    col = lax.broadcasted_iota(jnp.int32, (SUB, WIDTH), 1) % SUB
    diagonal = row == col
    row = lax.broadcasted_iota(jnp.int32, (BLOCK, WIDTH), 0) % SUB
    col = lax.broadcasted_iota(jnp.int32, (BLOCK, WIDTH), 1) % SUB
    differ = jnp.bitwise_xor(row, col)
    causal = row >= col
    head_row = lax.broadcasted_iota(jnp.int32, (PER_GROUP * SUB, WIDTH), 0) // SUB
    head_col = lax.broadcasted_iota(jnp.int32, (PER_GROUP * SUB, WIDTH), 1) // HEAD_DIM
    same_head = head_row == head_col
    spreads = [spread(128, level, LEVELS) for level in range(7)]
    subs = BLOCK // SUB

    @pl.loop(0, CHUNK // BLOCK)
    def _(k):
        first = k * BLOCK
        cum = cum_ref[pl.ds(first, BLOCK), :]
        x = load_x(ref, first, BLOCK)
        gates = gate_ref[pl.ds(first, BLOCK), :]
        dots = dot_nt(load_c(ref, first, BLOCK), load_b(ref, first, BLOCK))
        picked = dot(gates, spreads[6])
        for level in range(5, -1, -1):
            picked = jnp.where(differ < (1 << level), dot(gates, spreads[level]), picked)
        raw, gap = [], []
        for i in range(subs):
            rows = slice(i * SUB, (i + 1) * SUB)
            raw.append(jnp.concatenate([dots[rows, rows]] * PER_GROUP, axis=1))
            cum_row = jnp.sum(jnp.where(diagonal, cum[rows], 0.0), axis=0, keepdims=True)
            gap.append(cum[rows] - cum_row)
        decay = jnp.exp(jnp.minimum(jnp.concatenate(gap, axis=0), 0.0))
        raw = jnp.concatenate(raw, axis=0)
        scores = jnp.where(causal, raw * decay * picked, 0.0).astype(BF16)
        skip = gain * x.astype(F32)
        for i in range(subs):
            rows = slice(i * SUB, (i + 1) * SUB)
            tall_x = jnp.concatenate([x[rows]] * PER_GROUP, axis=0)
            block_x = jnp.where(same_head, tall_x, jnp.zeros_like(tall_x))
            out_ref[pl.ds(first + i * SUB, SUB), :] = dot(scores[rows], block_x) + skip[rows]


def near_part(received, cum, gain):
    return pl.pallas_call(
        near_kernel,
        out_shape=(
            jax.ShapeDtypeStruct((CHUNK, WIDTH), F32),
            jax.ShapeDtypeStruct((CHUNK, 128), BF16),
        ),
        scratch_shapes=[pltpu.VMEM((64, 16, 64), F32)],
        compiler_params=params(),
        cost_estimate=pl.CostEstimate(
            flops=4 * 10**9, bytes_accessed=4 * 1024 * 1024, transcendentals=10**6
        ),
        name="near_part",
    )(received, cum, gain)


def levels_kernel(ref, cum_ref, gate_ref, near_ref, own_ref, out_ref, grow_ref):
    subs = CHUNK // SUB
    starts = [jnp.zeros((1, WIDTH), F32)]
    starts += [cum_ref[i * SUB - 1 : i * SUB, :] for i in range(1, subs + 1)]
    states = []
    for i in range(subs):
        rows = slice(i * SUB, (i + 1) * SUB)
        cum = cum_ref[rows, :]
        tail = jnp.exp(starts[i + 1] - cum)
        high, low = halves(load_x(ref, i * SUB, SUB).astype(F32) * tail)
        b = load_b(ref, i * SUB, SUB)
        tall = jnp.concatenate([b, b], axis=0)
        states.append(dot_t(tall, jnp.concatenate([high, low], axis=0)))
        grow_ref[rows, :] = jnp.exp(cum - starts[i])
        out_ref[rows, :] = near_ref[rows, :]

    size = 1
    for bit in range(4):
        to_lanes = spread(128, 7 + bit, LEVELS)
        for group in range(1, subs // size, 2):
            rows = slice(group * size * SUB, (group + 1) * size * SUB)
            c = load_c(ref, rows.start, size * SUB)
            lower = jnp.concatenate(halves(states[group - 1]), axis=0)
            reached = dot(jnp.concatenate([c, c], axis=1), lower)
            gates = dot(gate_ref[rows, :], to_lanes)
            for part in range(size):
                i = group * size + part
                here = slice(i * SUB, (i + 1) * SUB)
                there = slice(part * SUB, (part + 1) * SUB)
                weight = gates[there] * grow_ref[here, :]
                if part:
                    weight = weight * jnp.exp(starts[i] - starts[group * size])
                out_ref[here, :] += weight * reached[there]
        states = [
            states[g] * jnp.exp(starts[(g + 2) * size] - starts[(g + 1) * size]) + states[g + 1]
            for g in range(0, subs // size, 2)
        ]
        size *= 2
    for i in range(1, subs):
        rows = slice(i * SUB, (i + 1) * SUB)
        grow_ref[rows, :] = grow_ref[rows, :] * jnp.exp(starts[i])


def levels_part(received, cum, gates, near, own):
    wide = jax.ShapeDtypeStruct((CHUNK, WIDTH), F32)
    vmem = pl.BlockSpec(memory_space=pltpu.VMEM)
    return pl.pallas_call(
        levels_kernel,
        in_specs=[vmem, vmem, vmem, vmem, pl.BlockSpec(memory_space=pl.ANY)],
        out_shape=(wide, wide),
        compiler_params=params(),
        cost_estimate=pl.CostEstimate(
            flops=4 * 10**9, bytes_accessed=4 * 1024 * 1024, transcendentals=10**6
        ),
        name="levels_part",
    )(received, cum, gates, near, own)


def outer_kernel(
    place_ref,
    ref,
    inner_ref,
    grow_ref,
    gate_ref,
    pair_ref,
    one_ref,
    two_ref,
    three_ref,
    out_ref,
):
    place = place_ref[0]
    in_half, odd, high = place % 2 == 1, place // 2 % 2 == 1, place // 4 == 1
    near_state, near_total = message_state(one_ref), message_total(one_ref)
    prefix = jnp.where(in_half, message_total(pair_ref), 0.0)
    far_prefix = prefix + jnp.where(odd, near_total, 0.0)
    late = jnp.where(odd, message_state(two_ref), near_state)
    late_total = jnp.where(odd, message_total(two_ref), near_total)
    early = jnp.where(odd, message_state(three_ref), message_state(two_ref))
    joined = jnp.exp(late_total) * early + late
    levels = (
        jnp.where(in_half, message_state(pair_ref), 0.0),
        jnp.where(odd, jnp.exp(prefix) * near_state, 0.0),
        jnp.where(high, jnp.exp(far_prefix) * joined, 0.0),
    )
    levels = [jnp.concatenate(halves(value), axis=0) for value in levels]
    spreads = [spread(128, 11 + bit, LEVELS) for bit in range(3)]
    for k in range(CHUNK // BLOCK):
        rows = slice(k * BLOCK, (k + 1) * BLOCK)
        c = load_c(ref, k * BLOCK, BLOCK)
        c = jnp.concatenate([c, c], axis=1)
        gates = gate_ref[rows, :]
        total = jnp.zeros((BLOCK, WIDTH), F32)
        for bit in range(3):
            total += dot(gates, spreads[bit]) * dot(c, levels[bit])
        mixed = inner_ref[rows, :] + grow_ref[rows, :] * total
        out_ref[k * 16 : (k + 1) * 16] = mixed.astype(BF16).reshape(BLOCK // 16, 16, WIDTH)


def outer_part(place, received, inner, grow, gates, messages):
    vmem = pl.BlockSpec(memory_space=pltpu.VMEM)
    return pl.pallas_call(
        outer_kernel,
        in_specs=[pl.BlockSpec(memory_space=pltpu.SMEM)] + [vmem] * 8,
        out_specs=vmem,
        out_shape=jax.ShapeDtypeStruct((64, 16, WIDTH), BF16),
        compiler_params=params(),
        name="outer_part",
    )(place, received, inner, grow, gates, *messages)


def unpack_kernel(place_ref, ref, out_ref, held_ref, sems):
    copies = []
    for k in range(SEQS):
        for g in range(GROUPS):
            held_ref[k, :, g * WIDTH : (g + 1) * WIDTH] = ref[k * GROUPS + g]
        copy = pltpu.make_async_copy(
            held_ref.at[k], out_ref.at[sequence_at(k, place_ref[0])], sems.at[k]
        )
        copy.start()
        copies.append(copy)
    for copy in copies:
        copy.wait()


def unpack(place, received):
    shape = (SEQS, 16, HEADS * HEAD_DIM)
    return pl.pallas_call(
        unpack_kernel,
        in_specs=[pl.BlockSpec(memory_space=pltpu.SMEM), pl.BlockSpec(memory_space=pltpu.VMEM)],
        out_specs=pl.BlockSpec(memory_space=pltpu.HBM),
        out_shape=jax.ShapeDtypeStruct(shape, BF16),
        scratch_shapes=[pltpu.VMEM(shape, BF16), pltpu.SemaphoreType.DMA((SEQS,))],
        compiler_params=params(),
        name="unpack_outputs",
    )(place, received)


def per_device(x_heads, b_keys, c_queries, log_decay, level_log, skip_gain):
    near_axes = ("block", "tp")
    place = lax.axis_index("chunk").astype(jnp.int32)[None]
    packed = pack(place, x_heads, b_keys, c_queries, log_decay, level_log)
    received = lax.all_to_all(packed, near_axes, 0, 0, tiled=True)
    gain = jnp.repeat(skip_gain, HEAD_DIM)[None, :]
    own, cum = chunk_state(received)
    pair = lax.ppermute(own, ("chunk", "block"), [(source, source ^ 6) for source in range(32)])
    near, gates = near_part(received, cum, gain)
    own = join(place, own, pair, near)
    shifted = [
        lax.ppermute(own, "chunk", [(source, source + 2 * z) for source in range(8 - 2 * z)])
        for z in (1, 2, 3)
    ]
    inner, grow = levels_part(received, cum, gates, near, own)
    mixed = outer_part(place, received, inner, grow, gates, [pair] + shifted)
    return unpack(place, lax.all_to_all(mixed, near_axes, 0, 0, tiled=True))


def solution(mesh):
    cut = Mesh(mesh.devices.reshape(8, 4, 16), ("chunk", "block", "tp"))
    split = P(None, ("chunk", "block", "tp"), None)
    return jax.shard_map(
        per_device,
        mesh=cut,
        in_specs=(split, split, split, split, split, P("tp")),
        out_specs=split,
        check_vma=False,
    )
```

```python
import jax
import jax.numpy as jnp
from jax import lax
from jax.experimental import pallas as pl
from jax.experimental.pallas import tpu as pltpu
from jax.sharding import Mesh
from jax.sharding import PartitionSpec as P

SEQS = 4
HEADS = 64
HEAD_DIM = 64
STATE = 128
GROUPS = 16
PER_GROUP = 4
LEVELS = 14
NEAR_LEVELS = 9
CHUNK = 1024
BLOCK = 256
SUB = 64
ROWS = 72
WIDTH = PER_GROUP * HEAD_DIM
GATES = PER_GROUP * LEVELS
CODE = 64.0
F32 = jnp.float32
BF16 = jnp.bfloat16
VMEM_LIMIT = 48 * 1024 * 1024


def dot(a, b):
    return jnp.dot(a, b, preferred_element_type=F32)


def dot_t(a, b):
    return lax.dot_general(a, b, (((0,), (0,)), ((), ())), preferred_element_type=F32)


def dot_nt(a, b):
    return lax.dot_general(a, b, (((1,), (1,)), ((), ())), preferred_element_type=F32)


def params():
    return pltpu.CompilerParams(vmem_limit_bytes=VMEM_LIMIT)


def pack_kernel(*refs):
    sources, out_ref = refs[:5], refs[5]
    x_ref, b_ref, c_ref, decay_ref, level_ref = held = refs[6:11]
    packed_ref, sems, out_sems = refs[11:]
    copies = [
        [
            pltpu.make_async_copy(source.at[k], slot.at[k], sems.at[i, k])
            for i, (source, slot) in enumerate(zip(sources, held))
        ]
        for k in range(SEQS)
    ]
    for group in copies:
        for copy in group:
            copy.start()
    sends = []
    for k, group in enumerate(copies):
        for copy in group:
            copy.wait()
        gates = jnp.exp(CODE * level_ref[k])
        decay = decay_ref[k]
        high = decay.astype(BF16).astype(F32)
        low = decay - high
        for g in range(GROUPS):
            at = k * GROUPS + g
            packed_ref[at, 0:16, :] = x_ref[k, :, g * WIDTH : g * WIDTH + 128]
            packed_ref[at, 16:32, :] = x_ref[k, :, g * WIDTH + 128 : (g + 1) * WIDTH]
            packed_ref[at, 32:48, :] = b_ref[k, :, g * STATE : (g + 1) * STATE]
            packed_ref[at, 48:64, :] = c_ref[k, :, g * STATE : (g + 1) * STATE]
            heads = slice(g * PER_GROUP, (g + 1) * PER_GROUP)
            piece = jnp.concatenate(
                [gates[:, g * GATES : (g + 1) * GATES], high[:, heads], low[:, heads]], axis=1
            )
            packed_ref[at, 64:72, :] = jnp.concatenate([piece[0:8], piece[8:16]], axis=1).astype(BF16)
        part = pl.ds(k * GROUPS, GROUPS)
        sends.append(
            pltpu.make_async_copy(packed_ref.at[part], out_ref.at[part], out_sems.at[k])
        )
        sends[-1].start()
    for copy in sends:
        copy.wait()


def pack(*arrays):
    shape = (SEQS * GROUPS, ROWS, 128)
    return pl.pallas_call(
        pack_kernel,
        in_specs=[pl.BlockSpec(memory_space=pltpu.HBM)] * len(arrays),
        out_specs=pl.BlockSpec(memory_space=pltpu.HBM),
        out_shape=jax.ShapeDtypeStruct(shape, BF16),
        scratch_shapes=[pltpu.VMEM(a.shape, a.dtype) for a in arrays]
        + [
            pltpu.VMEM(shape, BF16),
            pltpu.SemaphoreType.DMA((len(arrays), SEQS)),
            pltpu.SemaphoreType.DMA((SEQS,)),
        ],
        name="pack_messages",
    )(*arrays)


def load_rows(ref, first, count, start, stop):
    part = ref[pl.ds(first // 16, count // 16), start:stop, :]
    return part.reshape(count, 128)


def load_x(ref, first, count):
    return jnp.concatenate(
        [load_rows(ref, first, count, 0, 16), load_rows(ref, first, count, 16, 32)], axis=1
    )


def load_b(ref, first, count):
    return load_rows(ref, first, count, 32, 48)


def load_c(ref, first, count):
    return load_rows(ref, first, count, 48, 64)


def halves_wide(value):
    high = value.astype(BF16)
    return high, value - high.astype(F32)


def halves(value):
    high = value.astype(BF16)
    return high, (value - high.astype(F32)).astype(BF16)


def spread(rows, offset, stride):
    row = lax.broadcasted_iota(jnp.int32, (rows, WIDTH), 0) % 64
    head = lax.broadcasted_iota(jnp.int32, (rows, WIDTH), 1) // HEAD_DIM
    return jnp.where(row == offset + stride * head, 1.0, 0.0).astype(BF16)


def chunk_cumsum(ref, wide_ref, cum_ref):
    both = ref[:, 64:72, :].astype(F32)
    wide_ref[:, 0:8, :] = both[:, :, 0:64]
    wide_ref[:, 8:16, :] = both[:, :, 64:128]
    row = lax.broadcasted_iota(jnp.int32, (BLOCK, BLOCK), 0)
    col = lax.broadcasted_iota(jnp.int32, (BLOCK, BLOCK), 1)
    lower = jnp.where(row >= col, 1.0, 0.0).astype(BF16)
    lane = lax.broadcasted_iota(jnp.int32, (64, WIDTH), 0)
    head = lax.broadcasted_iota(jnp.int32, (64, WIDTH), 1) // HEAD_DIM
    wanted = (lane >= GATES) & (lane % PER_GROUP == head)
    widen = jnp.where(wanted, 1.0, 0.0).astype(BF16)
    widen = jnp.concatenate([widen] * 3, axis=0)
    offset = jnp.zeros((1, WIDTH), F32)
    for k in range(CHUNK // BLOCK):
        values = wide_ref[k * 16 : (k + 1) * 16].reshape(BLOCK, 64).astype(BF16)
        sums = dot(lower, values)
        high, rest = halves_wide(sums)
        middle, rest = halves_wide(rest)
        parts = jnp.concatenate([high, middle, rest.astype(BF16)], axis=1)
        cum = dot(parts, widen) + offset
        cum_ref[k * BLOCK : (k + 1) * BLOCK, :] = cum
        offset = cum[BLOCK - 1 :, :]
    return offset


def decode_gates(ref, wide_ref, gate_ref):
    both = ref[:, 64:72, :].astype(F32)
    lane = lax.broadcasted_iota(jnp.int32, both.shape, 2) % 64
    gates = jnp.exp(jnp.log(jnp.where(lane < GATES, both, 1.0)) * (1.0 / CODE))
    wide_ref[:, 0:8, :] = gates[:, :, 0:64]
    wide_ref[:, 8:16, :] = gates[:, :, 64:128]
    high, low = halves(wide_ref[...].reshape(CHUNK, 64))
    gate_ref[...] = jnp.concatenate([high, low], axis=1)


def split_rows(total):
    high = total.astype(BF16).astype(F32)
    middle = (total - high).astype(BF16).astype(F32)
    low = total - high - middle
    row = lax.broadcasted_iota(jnp.int32, (16, WIDTH), 0)
    rows = jnp.where(row == 0, high, jnp.where(row == 1, middle, jnp.where(row == 2, low, 0.0)))
    return rows.astype(BF16)


def message_state(ref):
    return ref[0:STATE, :].astype(F32)


def message_total(ref):
    rows = ref[STATE : STATE + 16, :].astype(F32)
    return rows[0:1] + rows[1:2] + rows[2:3]


def state_kernel(ref, out_ref, cum_ref, wide_ref):
    total = chunk_cumsum(ref, wide_ref, cum_ref)
    state = jnp.zeros((STATE, WIDTH), F32)
    for k in range(CHUNK // BLOCK):
        tail = jnp.exp(total - cum_ref[k * BLOCK : (k + 1) * BLOCK, :])
        high, low = halves(load_x(ref, k * BLOCK, BLOCK).astype(F32) * tail)
        b = load_b(ref, k * BLOCK, BLOCK)
        both = dot_t(b, jnp.concatenate([high, low], axis=1))
        state += both[:, :WIDTH] + both[:, WIDTH:]
    out_ref[0:STATE, :] = state.astype(BF16)
    out_ref[STATE : STATE + 16, :] = split_rows(total)


def chunk_state(received):
    return pl.pallas_call(
        state_kernel,
        out_shape=(
            jax.ShapeDtypeStruct((STATE + 16, WIDTH), BF16),
            jax.ShapeDtypeStruct((CHUNK, WIDTH), F32),
        ),
        scratch_shapes=[pltpu.VMEM((64, 16, 64), F32)],
        compiler_params=params(),
        name="chunk_state",
    )(received)


def join_kernel(place_ref, own_ref, partner_ref, near_ref, out_ref):
    upper = place_ref[0] % 2 == 1
    own, own_total = message_state(own_ref), message_total(own_ref)
    partner, partner_total = message_state(partner_ref), message_total(partner_ref)
    late_total = jnp.where(upper, own_total, partner_total)
    early = jnp.where(upper, partner, own)
    late = jnp.where(upper, own, partner)
    out_ref[0:STATE, :] = (jnp.exp(late_total) * early + late).astype(BF16)
    out_ref[STATE : STATE + 16, :] = split_rows(own_total + partner_total)


def join(place, own, partner, near):
    return pl.pallas_call(
        join_kernel,
        in_specs=[
            pl.BlockSpec(memory_space=pltpu.SMEM),
            pl.BlockSpec(memory_space=pltpu.VMEM),
            pl.BlockSpec(memory_space=pltpu.VMEM),
            pl.BlockSpec(memory_space=pl.ANY),
        ],
        out_shape=jax.ShapeDtypeStruct(own.shape, BF16),
        compiler_params=params(),
        name="join_states",
    )(place, own, partner, near)


def near_kernel(ref, cum_ref, gain_ref, out_ref, gate_ref, wide_ref):
    decode_gates(ref, wide_ref, gate_ref)
    gain = gain_ref[...]
    row = lax.broadcasted_iota(jnp.int32, (SUB, WIDTH), 0)
    col = lax.broadcasted_iota(jnp.int32, (SUB, WIDTH), 1) % SUB
    diagonal = row == col
    row = lax.broadcasted_iota(jnp.int32, (BLOCK, WIDTH), 0) % SUB
    col = lax.broadcasted_iota(jnp.int32, (BLOCK, WIDTH), 1) % SUB
    differ = jnp.bitwise_xor(row, col)
    causal = row >= col
    head_row = lax.broadcasted_iota(jnp.int32, (PER_GROUP * SUB, WIDTH), 0) // SUB
    head_col = lax.broadcasted_iota(jnp.int32, (PER_GROUP * SUB, WIDTH), 1) // HEAD_DIM
    same_head = head_row == head_col
    spreads = [spread(128, level, LEVELS) for level in range(7)]
    subs = BLOCK // SUB

    @pl.loop(0, CHUNK // BLOCK)
    def _(k):
        first = k * BLOCK
        cum = cum_ref[pl.ds(first, BLOCK), :]
        x = load_x(ref, first, BLOCK)
        gates = gate_ref[pl.ds(first, BLOCK), :]
        dots = dot_nt(load_c(ref, first, BLOCK), load_b(ref, first, BLOCK))
        picked = dot(gates, spreads[6])
        for level in range(5, -1, -1):
            picked = jnp.where(differ < (1 << level), dot(gates, spreads[level]), picked)
        raw, gap = [], []
        for i in range(subs):
            rows = slice(i * SUB, (i + 1) * SUB)
            raw.append(jnp.concatenate([dots[rows, rows]] * PER_GROUP, axis=1))
            cum_row = jnp.sum(jnp.where(diagonal, cum[rows], 0.0), axis=0, keepdims=True)
            gap.append(cum[rows] - cum_row)
        decay = jnp.exp(jnp.minimum(jnp.concatenate(gap, axis=0), 0.0))
        raw = jnp.concatenate(raw, axis=0)
        scores = jnp.where(causal, raw * decay * picked, 0.0).astype(BF16)
        skip = gain * x.astype(F32)
        for i in range(subs):
            rows = slice(i * SUB, (i + 1) * SUB)
            tall_x = jnp.concatenate([x[rows]] * PER_GROUP, axis=0)
            block_x = jnp.where(same_head, tall_x, jnp.zeros_like(tall_x))
            out_ref[pl.ds(first + i * SUB, SUB), :] = dot(scores[rows], block_x) + skip[rows]


def near_part(received, cum, gain):
    return pl.pallas_call(
        near_kernel,
        out_shape=(
            jax.ShapeDtypeStruct((CHUNK, WIDTH), F32),
            jax.ShapeDtypeStruct((CHUNK, 128), BF16),
        ),
        scratch_shapes=[pltpu.VMEM((64, 16, 64), F32)],
        compiler_params=params(),
        cost_estimate=pl.CostEstimate(
            flops=4 * 10**9, bytes_accessed=4 * 1024 * 1024, transcendentals=10**6
        ),
        name="near_part",
    )(received, cum, gain)


def levels_kernel(ref, cum_ref, gate_ref, near_ref, own_ref, out_ref, grow_ref):
    subs = CHUNK // SUB
    starts = [jnp.zeros((1, WIDTH), F32)]
    starts += [cum_ref[i * SUB - 1 : i * SUB, :] for i in range(1, subs + 1)]
    states = []
    for i in range(subs):
        rows = slice(i * SUB, (i + 1) * SUB)
        cum = cum_ref[rows, :]
        tail = jnp.exp(starts[i + 1] - cum)
        high, low = halves(load_x(ref, i * SUB, SUB).astype(F32) * tail)
        b = load_b(ref, i * SUB, SUB)
        tall = jnp.concatenate([b, b], axis=0)
        states.append(dot_t(tall, jnp.concatenate([high, low], axis=0)))
        grow_ref[rows, :] = jnp.exp(cum - starts[i])
        out_ref[rows, :] = near_ref[rows, :]

    size = 1
    for bit in range(4):
        to_lanes = spread(128, 7 + bit, LEVELS)
        for group in range(1, subs // size, 2):
            rows = slice(group * size * SUB, (group + 1) * size * SUB)
            c = load_c(ref, rows.start, size * SUB)
            lower = jnp.concatenate(halves(states[group - 1]), axis=0)
            reached = dot(jnp.concatenate([c, c], axis=1), lower)
            gates = dot(gate_ref[rows, :], to_lanes)
            for part in range(size):
                i = group * size + part
                here = slice(i * SUB, (i + 1) * SUB)
                there = slice(part * SUB, (part + 1) * SUB)
                weight = gates[there] * grow_ref[here, :]
                if part:
                    weight = weight * jnp.exp(starts[i] - starts[group * size])
                out_ref[here, :] += weight * reached[there]
        states = [
            states[g] * jnp.exp(starts[(g + 2) * size] - starts[(g + 1) * size]) + states[g + 1]
            for g in range(0, subs // size, 2)
        ]
        size *= 2
    for i in range(1, subs):
        rows = slice(i * SUB, (i + 1) * SUB)
        grow_ref[rows, :] = grow_ref[rows, :] * jnp.exp(starts[i])


def levels_part(received, cum, gates, near, own):
    wide = jax.ShapeDtypeStruct((CHUNK, WIDTH), F32)
    vmem = pl.BlockSpec(memory_space=pltpu.VMEM)
    return pl.pallas_call(
        levels_kernel,
        in_specs=[vmem, vmem, vmem, vmem, pl.BlockSpec(memory_space=pl.ANY)],
        out_shape=(wide, wide),
        compiler_params=params(),
        cost_estimate=pl.CostEstimate(
            flops=4 * 10**9, bytes_accessed=4 * 1024 * 1024, transcendentals=10**6
        ),
        name="levels_part",
    )(received, cum, gates, near, own)


def outer_kernel(
    place_ref,
    ref,
    inner_ref,
    grow_ref,
    gate_ref,
    pair_ref,
    top_ref,
    skip_ref,
    cross_ref,
    low_ref,
    out_ref,
):
    place = place_ref[0]
    in_half, odd = place % 2 == 1, place // 2 % 2 == 1
    prefix = jnp.where(in_half, message_total(pair_ref), 0.0)
    far_prefix = prefix + message_total(low_ref) + message_total(top_ref)
    cross, skip = message_state(cross_ref), message_state(skip_ref)
    late_total = jnp.where(odd, message_total(skip_ref), message_total(cross_ref))
    joined = jnp.exp(late_total) * jnp.where(odd, cross, skip) + jnp.where(odd, skip, cross)
    levels = (
        jnp.where(in_half, message_state(pair_ref), 0.0),
        jnp.exp(prefix) * (message_state(low_ref) + message_state(top_ref)),
        jnp.exp(far_prefix) * joined,
    )
    levels = [jnp.concatenate(halves(value), axis=0) for value in levels]
    spreads = [spread(128, 11 + bit, LEVELS) for bit in range(3)]
    for k in range(CHUNK // BLOCK):
        rows = slice(k * BLOCK, (k + 1) * BLOCK)
        c = load_c(ref, k * BLOCK, BLOCK)
        c = jnp.concatenate([c, c], axis=1)
        gates = gate_ref[rows, :]
        total = jnp.zeros((BLOCK, WIDTH), F32)
        for bit in range(3):
            total += dot(gates, spreads[bit]) * dot(c, levels[bit])
        mixed = inner_ref[rows, :] + grow_ref[rows, :] * total
        out_ref[k * 16 : (k + 1) * 16] = mixed.astype(BF16).reshape(BLOCK // 16, 16, WIDTH)


def outer_part(place, received, inner, grow, gates, messages):
    vmem = pl.BlockSpec(memory_space=pltpu.VMEM)
    return pl.pallas_call(
        outer_kernel,
        in_specs=[pl.BlockSpec(memory_space=pltpu.SMEM)] + [vmem] * 9,
        out_specs=vmem,
        out_shape=jax.ShapeDtypeStruct((64, 16, WIDTH), BF16),
        compiler_params=params(),
        name="outer_part",
    )(place, received, inner, grow, gates, *messages)


def unpack_kernel(ref, out_ref, held_ref, sems):
    copies = []
    for k in range(SEQS):
        for g in range(GROUPS):
            held_ref[k, :, g * WIDTH : (g + 1) * WIDTH] = ref[k * GROUPS + g]
        copy = pltpu.make_async_copy(held_ref.at[k], out_ref.at[k], sems.at[k])
        copy.start()
        copies.append(copy)
    for copy in copies:
        copy.wait()


def unpack(received):
    shape = (SEQS, 16, HEADS * HEAD_DIM)
    return pl.pallas_call(
        unpack_kernel,
        in_specs=[pl.BlockSpec(memory_space=pltpu.VMEM)],
        out_specs=pl.BlockSpec(memory_space=pltpu.HBM),
        out_shape=jax.ShapeDtypeStruct(shape, BF16),
        scratch_shapes=[pltpu.VMEM(shape, BF16), pltpu.SemaphoreType.DMA((SEQS,))],
        compiler_params=params(),
        name="unpack_outputs",
    )(received)


def per_device(x_heads, b_keys, c_queries, log_decay, level_log, skip_gain):
    near_axes = ("block", "tp")
    place = lax.axis_index("chunk").astype(jnp.int32)[None]
    packed = pack(x_heads, b_keys, c_queries, log_decay, level_log)
    received = lax.all_to_all(packed, near_axes, 0, 0, tiled=True)
    gain = jnp.repeat(skip_gain, HEAD_DIM)[None, :]
    own, cum = chunk_state(received)
    pair = lax.ppermute(own, "chunk", [(source, source ^ 1) for source in range(8)])
    near, gates = near_part(received, cum, gain)
    own = join(place, own, pair, near)
    steps = [[(2, 3)], [(0, 2), (1, 3)], [(0, 3), (1, 2)], [(0, 1)]]
    shared = [
        lax.ppermute(own, "chunk", [(2 * a + half, 2 * b + 1 - half) for a, b in step for half in (0, 1)])
        for step in steps
    ]
    inner, grow = levels_part(received, cum, gates, near, own)
    mixed = outer_part(place, received, inner, grow, gates, [pair] + shared)
    return unpack(lax.all_to_all(mixed, near_axes, 0, 0, tiled=True))


def solution(mesh):
    cut = Mesh(mesh.devices.reshape(8, 4, 16), ("chunk", "block", "tp"))
    split = P(None, ("chunk", "block", "tp"), None)
    return jax.shard_map(
        per_device,
        mesh=cut,
        in_specs=(split, split, split, split, split, P("tp")),
        out_specs=split,
        check_vma=False,
    )
```

```python
import jax
import jax.numpy as jnp
from jax import lax
from jax.experimental import pallas as pl
from jax.experimental.pallas import tpu as pltpu
from jax.sharding import Mesh
from jax.sharding import PartitionSpec as P

SEQS = 4
HEADS = 64
HEAD_DIM = 64
STATE = 128
GROUPS = 16
PER_GROUP = 4
LEVELS = 14
NEAR_LEVELS = 9
CHUNK = 1024
BLOCK = 256
SUB = 64
ROWS = 72
WIDTH = PER_GROUP * HEAD_DIM
GATES = PER_GROUP * LEVELS
CODE = 64.0
F32 = jnp.float32
BF16 = jnp.bfloat16
VMEM_LIMIT = 48 * 1024 * 1024


def dot(a, b):
    return jnp.dot(a, b, preferred_element_type=F32)


def dot_t(a, b):
    return lax.dot_general(a, b, (((0,), (0,)), ((), ())), preferred_element_type=F32)


def dot_nt(a, b):
    return lax.dot_general(a, b, (((1,), (1,)), ((), ())), preferred_element_type=F32)


def params():
    return pltpu.CompilerParams(vmem_limit_bytes=VMEM_LIMIT)


def pack_kernel(*refs):
    sources, out_ref = refs[:5], refs[5]
    x_ref, b_ref, c_ref, decay_ref, level_ref = held = refs[6:11]
    packed_ref, sems, out_sems = refs[11:]
    copies = [
        [
            pltpu.make_async_copy(source.at[k], slot.at[k], sems.at[i, k])
            for i, (source, slot) in enumerate(zip(sources, held))
        ]
        for k in range(SEQS)
    ]
    for group in copies:
        for copy in group:
            copy.start()
    sends = []
    for k, group in enumerate(copies):
        for copy in group:
            copy.wait()
        gates = jnp.exp(CODE * level_ref[k])
        decay = decay_ref[k]
        high = decay.astype(BF16).astype(F32)
        low = decay - high
        for g in range(GROUPS):
            at = k * GROUPS + g
            packed_ref[at, 0:16, :] = x_ref[k, :, g * WIDTH : g * WIDTH + 128]
            packed_ref[at, 16:32, :] = x_ref[k, :, g * WIDTH + 128 : (g + 1) * WIDTH]
            packed_ref[at, 32:48, :] = b_ref[k, :, g * STATE : (g + 1) * STATE]
            packed_ref[at, 48:64, :] = c_ref[k, :, g * STATE : (g + 1) * STATE]
            heads = slice(g * PER_GROUP, (g + 1) * PER_GROUP)
            piece = jnp.concatenate(
                [gates[:, g * GATES : (g + 1) * GATES], high[:, heads], low[:, heads]], axis=1
            )
            packed_ref[at, 64:72, :] = jnp.concatenate([piece[0:8], piece[8:16]], axis=1).astype(BF16)
        part = pl.ds(k * GROUPS, GROUPS)
        sends.append(
            pltpu.make_async_copy(packed_ref.at[part], out_ref.at[part], out_sems.at[k])
        )
        sends[-1].start()
    for copy in sends:
        copy.wait()


def pack(*arrays):
    shape = (SEQS * GROUPS, ROWS, 128)
    return pl.pallas_call(
        pack_kernel,
        in_specs=[pl.BlockSpec(memory_space=pltpu.HBM)] * len(arrays),
        out_specs=pl.BlockSpec(memory_space=pltpu.HBM),
        out_shape=jax.ShapeDtypeStruct(shape, BF16),
        scratch_shapes=[pltpu.VMEM(a.shape, a.dtype) for a in arrays]
        + [
            pltpu.VMEM(shape, BF16),
            pltpu.SemaphoreType.DMA((len(arrays), SEQS)),
            pltpu.SemaphoreType.DMA((SEQS,)),
        ],
        name="pack_messages",
    )(*arrays)


def load_rows(ref, first, count, start, stop):
    part = ref[pl.ds(first // 16, count // 16), start:stop, :]
    return part.reshape(count, 128)


def load_x(ref, first, count):
    return jnp.concatenate(
        [load_rows(ref, first, count, 0, 16), load_rows(ref, first, count, 16, 32)], axis=1
    )


def load_b(ref, first, count):
    return load_rows(ref, first, count, 32, 48)


def load_c(ref, first, count):
    return load_rows(ref, first, count, 48, 64)


def halves_wide(value):
    high = value.astype(BF16)
    return high, value - high.astype(F32)


def halves(value):
    high = value.astype(BF16)
    return high, (value - high.astype(F32)).astype(BF16)


def spread(rows, offset, stride):
    row = lax.broadcasted_iota(jnp.int32, (rows, WIDTH), 0) % 64
    head = lax.broadcasted_iota(jnp.int32, (rows, WIDTH), 1) // HEAD_DIM
    return jnp.where(row == offset + stride * head, 1.0, 0.0).astype(BF16)


def chunk_cumsum(ref, wide_ref, cum_ref):
    both = ref[:, 64:72, :].astype(F32)
    wide_ref[:, 0:8, :] = both[:, :, 0:64]
    wide_ref[:, 8:16, :] = both[:, :, 64:128]
    row = lax.broadcasted_iota(jnp.int32, (BLOCK, BLOCK), 0)
    col = lax.broadcasted_iota(jnp.int32, (BLOCK, BLOCK), 1)
    lower = jnp.where(row >= col, 1.0, 0.0).astype(BF16)
    lane = lax.broadcasted_iota(jnp.int32, (64, WIDTH), 0)
    head = lax.broadcasted_iota(jnp.int32, (64, WIDTH), 1) // HEAD_DIM
    wanted = (lane >= GATES) & (lane % PER_GROUP == head)
    widen = jnp.where(wanted, 1.0, 0.0).astype(BF16)
    widen = jnp.concatenate([widen] * 3, axis=0)
    offset = jnp.zeros((1, WIDTH), F32)
    for k in range(CHUNK // BLOCK):
        values = wide_ref[k * 16 : (k + 1) * 16].reshape(BLOCK, 64).astype(BF16)
        sums = dot(lower, values)
        high, rest = halves_wide(sums)
        middle, rest = halves_wide(rest)
        parts = jnp.concatenate([high, middle, rest.astype(BF16)], axis=1)
        cum = dot(parts, widen) + offset
        cum_ref[k * BLOCK : (k + 1) * BLOCK, :] = cum
        offset = cum[BLOCK - 1 :, :]
    return offset


def decode_gates(ref, wide_ref, gate_ref):
    both = ref[:, 64:72, :].astype(F32)
    lane = lax.broadcasted_iota(jnp.int32, both.shape, 2) % 64
    gates = jnp.exp(jnp.log(jnp.where(lane < GATES, both, 1.0)) * (1.0 / CODE))
    wide_ref[:, 0:8, :] = gates[:, :, 0:64]
    wide_ref[:, 8:16, :] = gates[:, :, 64:128]
    high, low = halves(wide_ref[...].reshape(CHUNK, 64))
    gate_ref[...] = jnp.concatenate([high, low], axis=1)


def split_rows(total):
    high = total.astype(BF16).astype(F32)
    middle = (total - high).astype(BF16).astype(F32)
    low = total - high - middle
    row = lax.broadcasted_iota(jnp.int32, (16, WIDTH), 0)
    rows = jnp.where(row == 0, high, jnp.where(row == 1, middle, jnp.where(row == 2, low, 0.0)))
    return rows.astype(BF16)


def message_state(ref):
    return ref[0:STATE, :].astype(F32)


def message_total(ref):
    rows = ref[STATE : STATE + 16, :].astype(F32)
    return rows[0:1] + rows[1:2] + rows[2:3]


def state_kernel(ref, out_ref, cum_ref, wide_ref):
    total = chunk_cumsum(ref, wide_ref, cum_ref)
    state = jnp.zeros((STATE, WIDTH), F32)
    for k in range(CHUNK // BLOCK):
        tail = jnp.exp(total - cum_ref[k * BLOCK : (k + 1) * BLOCK, :])
        high, low = halves(load_x(ref, k * BLOCK, BLOCK).astype(F32) * tail)
        b = load_b(ref, k * BLOCK, BLOCK)
        both = dot_t(b, jnp.concatenate([high, low], axis=1))
        state += both[:, :WIDTH] + both[:, WIDTH:]
    out_ref[0:STATE, :] = state.astype(BF16)
    out_ref[STATE : STATE + 16, :] = split_rows(total)


def chunk_state(received):
    return pl.pallas_call(
        state_kernel,
        out_shape=(
            jax.ShapeDtypeStruct((STATE + 16, WIDTH), BF16),
            jax.ShapeDtypeStruct((CHUNK, WIDTH), F32),
        ),
        scratch_shapes=[pltpu.VMEM((64, 16, 64), F32)],
        compiler_params=params(),
        name="chunk_state",
    )(received)


def join_kernel(place_ref, own_ref, partner_ref, near_ref, out_ref):
    upper = place_ref[0] % 2 == 1
    own, own_total = message_state(own_ref), message_total(own_ref)
    partner, partner_total = message_state(partner_ref), message_total(partner_ref)
    late_total = jnp.where(upper, own_total, partner_total)
    early = jnp.where(upper, partner, own)
    late = jnp.where(upper, own, partner)
    out_ref[0:STATE, :] = (jnp.exp(late_total) * early + late).astype(BF16)
    out_ref[STATE : STATE + 16, :] = split_rows(own_total + partner_total)


def join(place, own, partner, near):
    return pl.pallas_call(
        join_kernel,
        in_specs=[
            pl.BlockSpec(memory_space=pltpu.SMEM),
            pl.BlockSpec(memory_space=pltpu.VMEM),
            pl.BlockSpec(memory_space=pltpu.VMEM),
            pl.BlockSpec(memory_space=pl.ANY),
        ],
        out_shape=jax.ShapeDtypeStruct(own.shape, BF16),
        compiler_params=params(),
        name="join_states",
    )(place, own, partner, near)


def relay_kernel(before_ref, first_ref, inner_ref, out_ref):
    total = message_total(before_ref)
    state = jnp.exp(total) * message_state(first_ref) + message_state(before_ref)
    out_ref[0:STATE, :] = state.astype(BF16)
    out_ref[STATE : STATE + 16, :] = split_rows(total + message_total(first_ref))


def relay(before, first, inner):
    vmem = pl.BlockSpec(memory_space=pltpu.VMEM)
    return pl.pallas_call(
        relay_kernel,
        in_specs=[vmem, vmem, pl.BlockSpec(memory_space=pl.ANY)],
        out_shape=jax.ShapeDtypeStruct(before.shape, BF16),
        compiler_params=params(),
        name="relay_states",
    )(before, first, inner)


def near_kernel(ref, cum_ref, gain_ref, out_ref, gate_ref, wide_ref):
    decode_gates(ref, wide_ref, gate_ref)
    gain = gain_ref[...]
    row = lax.broadcasted_iota(jnp.int32, (SUB, WIDTH), 0)
    col = lax.broadcasted_iota(jnp.int32, (SUB, WIDTH), 1) % SUB
    diagonal = row == col
    row = lax.broadcasted_iota(jnp.int32, (BLOCK, WIDTH), 0) % SUB
    col = lax.broadcasted_iota(jnp.int32, (BLOCK, WIDTH), 1) % SUB
    differ = jnp.bitwise_xor(row, col)
    causal = row >= col
    head_row = lax.broadcasted_iota(jnp.int32, (PER_GROUP * SUB, WIDTH), 0) // SUB
    head_col = lax.broadcasted_iota(jnp.int32, (PER_GROUP * SUB, WIDTH), 1) // HEAD_DIM
    same_head = head_row == head_col
    spreads = [spread(128, level, LEVELS) for level in range(7)]
    subs = BLOCK // SUB

    @pl.loop(0, CHUNK // BLOCK)
    def _(k):
        first = k * BLOCK
        cum = cum_ref[pl.ds(first, BLOCK), :]
        x = load_x(ref, first, BLOCK)
        gates = gate_ref[pl.ds(first, BLOCK), :]
        dots = dot_nt(load_c(ref, first, BLOCK), load_b(ref, first, BLOCK))
        picked = dot(gates, spreads[6])
        for level in range(5, -1, -1):
            picked = jnp.where(differ < (1 << level), dot(gates, spreads[level]), picked)
        raw, gap = [], []
        for i in range(subs):
            rows = slice(i * SUB, (i + 1) * SUB)
            raw.append(jnp.concatenate([dots[rows, rows]] * PER_GROUP, axis=1))
            cum_row = jnp.sum(jnp.where(diagonal, cum[rows], 0.0), axis=0, keepdims=True)
            gap.append(cum[rows] - cum_row)
        decay = jnp.exp(jnp.minimum(jnp.concatenate(gap, axis=0), 0.0))
        raw = jnp.concatenate(raw, axis=0)
        scores = jnp.where(causal, raw * decay * picked, 0.0).astype(BF16)
        skip = gain * x.astype(F32)
        for i in range(subs):
            rows = slice(i * SUB, (i + 1) * SUB)
            tall_x = jnp.concatenate([x[rows]] * PER_GROUP, axis=0)
            block_x = jnp.where(same_head, tall_x, jnp.zeros_like(tall_x))
            out_ref[pl.ds(first + i * SUB, SUB), :] = dot(scores[rows], block_x) + skip[rows]


def near_part(received, cum, gain):
    return pl.pallas_call(
        near_kernel,
        out_shape=(
            jax.ShapeDtypeStruct((CHUNK, WIDTH), F32),
            jax.ShapeDtypeStruct((CHUNK, 128), BF16),
        ),
        scratch_shapes=[pltpu.VMEM((64, 16, 64), F32)],
        compiler_params=params(),
        cost_estimate=pl.CostEstimate(
            flops=4 * 10**9, bytes_accessed=4 * 1024 * 1024, transcendentals=10**6
        ),
        name="near_part",
    )(received, cum, gain)


def levels_kernel(ref, cum_ref, gate_ref, near_ref, own_ref, out_ref, grow_ref, copy_ref):
    copy_ref[...] = own_ref[...]
    subs = CHUNK // SUB
    starts = [jnp.zeros((1, WIDTH), F32)]
    starts += [cum_ref[i * SUB - 1 : i * SUB, :] for i in range(1, subs + 1)]
    states = []
    for i in range(subs):
        rows = slice(i * SUB, (i + 1) * SUB)
        cum = cum_ref[rows, :]
        tail = jnp.exp(starts[i + 1] - cum)
        high, low = halves(load_x(ref, i * SUB, SUB).astype(F32) * tail)
        b = load_b(ref, i * SUB, SUB)
        tall = jnp.concatenate([b, b], axis=0)
        states.append(dot_t(tall, jnp.concatenate([high, low], axis=0)))
        grow_ref[rows, :] = jnp.exp(cum - starts[i])
        out_ref[rows, :] = near_ref[rows, :]

    size = 1
    for bit in range(4):
        to_lanes = spread(128, 7 + bit, LEVELS)
        for group in range(1, subs // size, 2):
            rows = slice(group * size * SUB, (group + 1) * size * SUB)
            c = load_c(ref, rows.start, size * SUB)
            lower = jnp.concatenate(halves(states[group - 1]), axis=0)
            reached = dot(jnp.concatenate([c, c], axis=1), lower)
            gates = dot(gate_ref[rows, :], to_lanes)
            for part in range(size):
                i = group * size + part
                here = slice(i * SUB, (i + 1) * SUB)
                there = slice(part * SUB, (part + 1) * SUB)
                weight = gates[there] * grow_ref[here, :]
                if part:
                    weight = weight * jnp.exp(starts[i] - starts[group * size])
                out_ref[here, :] += weight * reached[there]
        states = [
            states[g] * jnp.exp(starts[(g + 2) * size] - starts[(g + 1) * size]) + states[g + 1]
            for g in range(0, subs // size, 2)
        ]
        size *= 2
    for i in range(1, subs):
        rows = slice(i * SUB, (i + 1) * SUB)
        grow_ref[rows, :] = grow_ref[rows, :] * jnp.exp(starts[i])


def levels_part(received, cum, gates, near, own):
    wide = jax.ShapeDtypeStruct((CHUNK, WIDTH), F32)
    vmem = pl.BlockSpec(memory_space=pltpu.VMEM)
    return pl.pallas_call(
        levels_kernel,
        in_specs=[vmem] * 5,
        out_shape=(wide, wide, jax.ShapeDtypeStruct(own.shape, BF16)),
        compiler_params=params(),
        cost_estimate=pl.CostEstimate(
            flops=4 * 10**9, bytes_accessed=4 * 1024 * 1024, transcendentals=10**6
        ),
        name="levels_part",
    )(received, cum, gates, near, own)


def outer_kernel(
    place_ref,
    ref,
    inner_ref,
    grow_ref,
    gate_ref,
    pair_ref,
    before_ref,
    last_ref,
    own_far_ref,
    far_ref,
    out_ref,
):
    place = place_ref[0]
    in_half, one, two = place % 2 == 1, place // 2 == 1, place // 2 == 2
    prefix = jnp.where(in_half, message_total(pair_ref), 0.0)
    far_prefix = prefix + message_total(last_ref)
    levels = (
        jnp.where(in_half, message_state(pair_ref), 0.0),
        jnp.exp(prefix) * jnp.where(one, message_state(before_ref), message_state(last_ref)),
        jnp.exp(far_prefix) * jnp.where(two, message_state(own_far_ref), message_state(far_ref)),
    )
    levels = [jnp.concatenate(halves(value), axis=0) for value in levels]
    spreads = [spread(128, 11 + bit, LEVELS) for bit in range(3)]
    for k in range(CHUNK // BLOCK):
        rows = slice(k * BLOCK, (k + 1) * BLOCK)
        c = load_c(ref, k * BLOCK, BLOCK)
        c = jnp.concatenate([c, c], axis=1)
        gates = gate_ref[rows, :]
        total = jnp.zeros((BLOCK, WIDTH), F32)
        for bit in range(3):
            total += dot(gates, spreads[bit]) * dot(c, levels[bit])
        mixed = inner_ref[rows, :] + grow_ref[rows, :] * total
        out_ref[k * 16 : (k + 1) * 16] = mixed.astype(BF16).reshape(BLOCK // 16, 16, WIDTH)


def outer_part(place, received, inner, grow, gates, messages):
    vmem = pl.BlockSpec(memory_space=pltpu.VMEM)
    return pl.pallas_call(
        outer_kernel,
        in_specs=[pl.BlockSpec(memory_space=pltpu.SMEM)] + [vmem] * 9,
        out_specs=vmem,
        out_shape=jax.ShapeDtypeStruct((64, 16, WIDTH), BF16),
        compiler_params=params(),
        name="outer_part",
    )(place, received, inner, grow, gates, *messages)


def unpack_kernel(ref, out_ref, held_ref, sems):
    copies = []
    for k in range(SEQS):
        for g in range(GROUPS):
            held_ref[k, :, g * WIDTH : (g + 1) * WIDTH] = ref[k * GROUPS + g]
        copy = pltpu.make_async_copy(held_ref.at[k], out_ref.at[k], sems.at[k])
        copy.start()
        copies.append(copy)
    for copy in copies:
        copy.wait()


def unpack(received):
    shape = (SEQS, 16, HEADS * HEAD_DIM)
    return pl.pallas_call(
        unpack_kernel,
        in_specs=[pl.BlockSpec(memory_space=pltpu.VMEM)],
        out_specs=pl.BlockSpec(memory_space=pltpu.HBM),
        out_shape=jax.ShapeDtypeStruct(shape, BF16),
        scratch_shapes=[pltpu.VMEM(shape, BF16), pltpu.SemaphoreType.DMA((SEQS,))],
        compiler_params=params(),
        name="unpack_outputs",
    )(received)


def per_device(x_heads, b_keys, c_queries, log_decay, level_log, skip_gain):
    near_axes = ("block", "tp")
    place = lax.axis_index("chunk").astype(jnp.int32)[None]
    packed = pack(x_heads, b_keys, c_queries, log_decay, level_log)
    received = lax.all_to_all(packed, near_axes, 0, 0, tiled=True)
    gain = jnp.repeat(skip_gain, HEAD_DIM)[None, :]
    own, cum = chunk_state(received)
    pair = lax.ppermute(own, "chunk", [(source, source ^ 1) for source in range(8)])
    near, gates = near_part(received, cum, gain)
    own = join(place, own, pair, near)

    def up(value, step):
        pairs = [(2 * a + half, 2 * b + 1 - half) for a, b in step for half in (0, 1)]
        return lax.ppermute(value, "chunk", pairs)

    first = up(own, [(0, 2)])
    before = up(own, [(0, 1), (1, 2)])
    inner, grow, later = levels_part(received, cum, gates, near, own)
    last = up(later, [(2, 3)])
    own_far = relay(before, first, inner)
    far = up(own_far, [(2, 3)])
    shared = [before, last, own_far, far]
    mixed = outer_part(place, received, inner, grow, gates, [pair] + shared)
    return unpack(lax.all_to_all(mixed, near_axes, 0, 0, tiled=True))


def solution(mesh):
    cut = Mesh(mesh.devices.reshape(8, 4, 16), ("chunk", "block", "tp"))
    split = P(None, ("chunk", "block", "tp"), None)
    return jax.shard_map(
        per_device,
        mesh=cut,
        in_specs=(split, split, split, split, split, P("tp")),
        out_specs=split,
        check_vma=False,
    )
```

```python
import jax
import jax.numpy as jnp
from jax import lax
from jax.experimental import pallas as pl
from jax.experimental.pallas import tpu as pltpu
from jax.sharding import Mesh
from jax.sharding import PartitionSpec as P

SEQS = 4
HEADS = 64
HEAD_DIM = 64
STATE = 128
GROUPS = 16
PER_GROUP = 4
LEVELS = 14
NEAR_LEVELS = 9
CHUNK = 1024
BLOCK = 256
SUB = 64
ROWS = 72
WIDTH = PER_GROUP * HEAD_DIM
GATES = PER_GROUP * LEVELS
CODE = 64.0
F32 = jnp.float32
BF16 = jnp.bfloat16
VMEM_LIMIT = 48 * 1024 * 1024


def dot(a, b):
    return jnp.dot(a, b, preferred_element_type=F32)


def dot_t(a, b):
    return lax.dot_general(a, b, (((0,), (0,)), ((), ())), preferred_element_type=F32)


def dot_nt(a, b):
    return lax.dot_general(a, b, (((1,), (1,)), ((), ())), preferred_element_type=F32)


def params():
    return pltpu.CompilerParams(vmem_limit_bytes=VMEM_LIMIT)


def pack_kernel(*refs):
    sources, out_ref = refs[:5], refs[5]
    x_ref, b_ref, c_ref, decay_ref, level_ref = held = refs[6:11]
    packed_ref, sems, out_sems = refs[11:]
    copies = [
        [
            pltpu.make_async_copy(source.at[k], slot.at[k], sems.at[i, k])
            for i, (source, slot) in enumerate(zip(sources, held))
        ]
        for k in range(SEQS)
    ]
    for group in copies:
        for copy in group:
            copy.start()
    sends = []
    for k, group in enumerate(copies):
        for copy in group:
            copy.wait()
        gates = jnp.exp(CODE * level_ref[k])
        decay = decay_ref[k]
        high = decay.astype(BF16).astype(F32)
        low = decay - high
        for g in range(GROUPS):
            at = k * GROUPS + g
            packed_ref[at, 0:16, :] = x_ref[k, :, g * WIDTH : g * WIDTH + 128]
            packed_ref[at, 16:32, :] = x_ref[k, :, g * WIDTH + 128 : (g + 1) * WIDTH]
            packed_ref[at, 32:48, :] = b_ref[k, :, g * STATE : (g + 1) * STATE]
            packed_ref[at, 48:64, :] = c_ref[k, :, g * STATE : (g + 1) * STATE]
            heads = slice(g * PER_GROUP, (g + 1) * PER_GROUP)
            piece = jnp.concatenate(
                [gates[:, g * GATES : (g + 1) * GATES], high[:, heads], low[:, heads]], axis=1
            )
            packed_ref[at, 64:72, :] = jnp.concatenate([piece[0:8], piece[8:16]], axis=1).astype(BF16)
        part = pl.ds(k * GROUPS, GROUPS)
        sends.append(
            pltpu.make_async_copy(packed_ref.at[part], out_ref.at[part], out_sems.at[k])
        )
        sends[-1].start()
    for copy in sends:
        copy.wait()


def pack(*arrays):
    shape = (SEQS * GROUPS, ROWS, 128)
    return pl.pallas_call(
        pack_kernel,
        in_specs=[pl.BlockSpec(memory_space=pltpu.HBM)] * len(arrays),
        out_specs=pl.BlockSpec(memory_space=pltpu.HBM),
        out_shape=jax.ShapeDtypeStruct(shape, BF16),
        scratch_shapes=[pltpu.VMEM(a.shape, a.dtype) for a in arrays]
        + [
            pltpu.VMEM(shape, BF16),
            pltpu.SemaphoreType.DMA((len(arrays), SEQS)),
            pltpu.SemaphoreType.DMA((SEQS,)),
        ],
        name="pack_messages",
    )(*arrays)


def load_rows(ref, first, count, start, stop):
    part = ref[pl.ds(first // 16, count // 16), start:stop, :]
    return part.reshape(count, 128)


def load_x(ref, first, count):
    return jnp.concatenate(
        [load_rows(ref, first, count, 0, 16), load_rows(ref, first, count, 16, 32)], axis=1
    )


def load_b(ref, first, count):
    return load_rows(ref, first, count, 32, 48)


def load_c(ref, first, count):
    return load_rows(ref, first, count, 48, 64)


def halves_wide(value):
    high = value.astype(BF16)
    return high, value - high.astype(F32)


def halves(value):
    high = value.astype(BF16)
    return high, (value - high.astype(F32)).astype(BF16)


def spread(rows, offset, stride):
    row = lax.broadcasted_iota(jnp.int32, (rows, WIDTH), 0) % 64
    head = lax.broadcasted_iota(jnp.int32, (rows, WIDTH), 1) // HEAD_DIM
    return jnp.where(row == offset + stride * head, 1.0, 0.0).astype(BF16)


def chunk_cumsum(ref, wide_ref, cum_ref):
    both = ref[:, 64:72, :].astype(F32)
    wide_ref[:, 0:8, :] = both[:, :, 0:64]
    wide_ref[:, 8:16, :] = both[:, :, 64:128]
    row = lax.broadcasted_iota(jnp.int32, (BLOCK, BLOCK), 0)
    col = lax.broadcasted_iota(jnp.int32, (BLOCK, BLOCK), 1)
    lower = jnp.where(row >= col, 1.0, 0.0).astype(BF16)
    lane = lax.broadcasted_iota(jnp.int32, (64, WIDTH), 0)
    head = lax.broadcasted_iota(jnp.int32, (64, WIDTH), 1) // HEAD_DIM
    wanted = (lane >= GATES) & (lane % PER_GROUP == head)
    widen = jnp.where(wanted, 1.0, 0.0).astype(BF16)
    widen = jnp.concatenate([widen] * 3, axis=0)
    offset = jnp.zeros((1, WIDTH), F32)
    for k in range(CHUNK // BLOCK):
        values = wide_ref[k * 16 : (k + 1) * 16].reshape(BLOCK, 64).astype(BF16)
        sums = dot(lower, values)
        high, rest = halves_wide(sums)
        middle, rest = halves_wide(rest)
        parts = jnp.concatenate([high, middle, rest.astype(BF16)], axis=1)
        cum = dot(parts, widen) + offset
        cum_ref[k * BLOCK : (k + 1) * BLOCK, :] = cum
        offset = cum[BLOCK - 1 :, :]
    return offset


def decode_gates(ref, wide_ref, gate_ref):
    both = ref[:, 64:72, :].astype(F32)
    lane = lax.broadcasted_iota(jnp.int32, both.shape, 2) % 64
    gates = jnp.exp(jnp.log(jnp.where(lane < GATES, both, 1.0)) * (1.0 / CODE))
    wide_ref[:, 0:8, :] = gates[:, :, 0:64]
    wide_ref[:, 8:16, :] = gates[:, :, 64:128]
    high, low = halves(wide_ref[...].reshape(CHUNK, 64))
    gate_ref[...] = jnp.concatenate([high, low], axis=1)


def split_rows(total):
    high = total.astype(BF16).astype(F32)
    middle = (total - high).astype(BF16).astype(F32)
    low = total - high - middle
    row = lax.broadcasted_iota(jnp.int32, (16, WIDTH), 0)
    rows = jnp.where(row == 0, high, jnp.where(row == 1, middle, jnp.where(row == 2, low, 0.0)))
    return rows.astype(BF16)


def message_state(ref):
    return ref[0:STATE, :].astype(F32)


def message_total(ref):
    rows = ref[STATE : STATE + 16, :].astype(F32)
    return rows[0:1] + rows[1:2] + rows[2:3]


def state_kernel(ref, out_ref, cum_ref, wide_ref):
    total = chunk_cumsum(ref, wide_ref, cum_ref)
    state = jnp.zeros((STATE, WIDTH), F32)
    for k in range(CHUNK // BLOCK):
        tail = jnp.exp(total - cum_ref[k * BLOCK : (k + 1) * BLOCK, :])
        high, low = halves(load_x(ref, k * BLOCK, BLOCK).astype(F32) * tail)
        b = load_b(ref, k * BLOCK, BLOCK)
        both = dot_t(b, jnp.concatenate([high, low], axis=1))
        state += both[:, :WIDTH] + both[:, WIDTH:]
    out_ref[0:STATE, :] = state.astype(BF16)
    out_ref[STATE : STATE + 16, :] = split_rows(total)


def chunk_state(received):
    return pl.pallas_call(
        state_kernel,
        out_shape=(
            jax.ShapeDtypeStruct((STATE + 16, WIDTH), BF16),
            jax.ShapeDtypeStruct((CHUNK, WIDTH), F32),
        ),
        scratch_shapes=[pltpu.VMEM((64, 16, 64), F32)],
        compiler_params=params(),
        name="chunk_state",
    )(received)


def join_kernel(place_ref, own_ref, partner_ref, near_ref, out_ref):
    upper = place_ref[0] % 2 == 1
    own, own_total = message_state(own_ref), message_total(own_ref)
    partner, partner_total = message_state(partner_ref), message_total(partner_ref)
    late_total = jnp.where(upper, own_total, partner_total)
    early = jnp.where(upper, partner, own)
    late = jnp.where(upper, own, partner)
    out_ref[0:STATE, :] = (jnp.exp(late_total) * early + late).astype(BF16)
    out_ref[STATE : STATE + 16, :] = split_rows(own_total + partner_total)


def join(place, own, partner, near):
    return pl.pallas_call(
        join_kernel,
        in_specs=[
            pl.BlockSpec(memory_space=pltpu.SMEM),
            pl.BlockSpec(memory_space=pltpu.VMEM),
            pl.BlockSpec(memory_space=pltpu.VMEM),
            pl.BlockSpec(memory_space=pl.ANY),
        ],
        out_shape=jax.ShapeDtypeStruct(own.shape, BF16),
        compiler_params=params(),
        name="join_states",
    )(place, own, partner, near)


def relay_kernel(place_ref, own_ref, before_ref, inner_ref, out_ref, shift_ref):
    total = message_total(own_ref)
    state = jnp.exp(total) * message_state(before_ref) + message_state(own_ref)
    out_ref[0:STATE, :] = state.astype(BF16)
    out_ref[STATE : STATE + 16, :] = split_rows(total + message_total(before_ref))
    shift_ref[...] = jnp.where(place_ref[0] // 2 == 2, own_ref[...], out_ref[...])


def relay(place, own, before, inner):
    vmem = pl.BlockSpec(memory_space=pltpu.VMEM)
    message = jax.ShapeDtypeStruct(own.shape, BF16)
    return pl.pallas_call(
        relay_kernel,
        in_specs=[
            pl.BlockSpec(memory_space=pltpu.SMEM),
            vmem,
            vmem,
            pl.BlockSpec(memory_space=pl.ANY),
        ],
        out_shape=(message, message),
        compiler_params=params(),
        name="relay_states",
    )(place, own, before, inner)


def near_kernel(ref, cum_ref, gain_ref, out_ref, gate_ref, wide_ref):
    decode_gates(ref, wide_ref, gate_ref)
    gain = gain_ref[...]
    row = lax.broadcasted_iota(jnp.int32, (SUB, WIDTH), 0)
    col = lax.broadcasted_iota(jnp.int32, (SUB, WIDTH), 1) % SUB
    diagonal = row == col
    row = lax.broadcasted_iota(jnp.int32, (BLOCK, WIDTH), 0) % SUB
    col = lax.broadcasted_iota(jnp.int32, (BLOCK, WIDTH), 1) % SUB
    differ = jnp.bitwise_xor(row, col)
    causal = row >= col
    head_row = lax.broadcasted_iota(jnp.int32, (PER_GROUP * SUB, WIDTH), 0) // SUB
    head_col = lax.broadcasted_iota(jnp.int32, (PER_GROUP * SUB, WIDTH), 1) // HEAD_DIM
    same_head = head_row == head_col
    spreads = [spread(128, level, LEVELS) for level in range(7)]
    subs = BLOCK // SUB

    @pl.loop(0, CHUNK // BLOCK)
    def _(k):
        first = k * BLOCK
        cum = cum_ref[pl.ds(first, BLOCK), :]
        x = load_x(ref, first, BLOCK)
        gates = gate_ref[pl.ds(first, BLOCK), :]
        dots = dot_nt(load_c(ref, first, BLOCK), load_b(ref, first, BLOCK))
        picked = dot(gates, spreads[6])
        for level in range(5, -1, -1):
            picked = jnp.where(differ < (1 << level), dot(gates, spreads[level]), picked)
        raw, gap = [], []
        for i in range(subs):
            rows = slice(i * SUB, (i + 1) * SUB)
            raw.append(jnp.concatenate([dots[rows, rows]] * PER_GROUP, axis=1))
            cum_row = jnp.sum(jnp.where(diagonal, cum[rows], 0.0), axis=0, keepdims=True)
            gap.append(cum[rows] - cum_row)
        decay = jnp.exp(jnp.minimum(jnp.concatenate(gap, axis=0), 0.0))
        raw = jnp.concatenate(raw, axis=0)
        scores = jnp.where(causal, raw * decay * picked, 0.0).astype(BF16)
        skip = gain * x.astype(F32)
        for i in range(subs):
            rows = slice(i * SUB, (i + 1) * SUB)
            tall_x = jnp.concatenate([x[rows]] * PER_GROUP, axis=0)
            block_x = jnp.where(same_head, tall_x, jnp.zeros_like(tall_x))
            out_ref[pl.ds(first + i * SUB, SUB), :] = dot(scores[rows], block_x) + skip[rows]


def near_part(received, cum, gain):
    return pl.pallas_call(
        near_kernel,
        out_shape=(
            jax.ShapeDtypeStruct((CHUNK, WIDTH), F32),
            jax.ShapeDtypeStruct((CHUNK, 128), BF16),
        ),
        scratch_shapes=[pltpu.VMEM((64, 16, 64), F32)],
        compiler_params=params(),
        cost_estimate=pl.CostEstimate(
            flops=4 * 10**9, bytes_accessed=4 * 1024 * 1024, transcendentals=10**6
        ),
        name="near_part",
    )(received, cum, gain)


def levels_kernel(ref, cum_ref, gate_ref, near_ref, own_ref, out_ref, grow_ref):
    subs = CHUNK // SUB
    starts = [jnp.zeros((1, WIDTH), F32)]
    starts += [cum_ref[i * SUB - 1 : i * SUB, :] for i in range(1, subs + 1)]
    states = []
    for i in range(subs):
        rows = slice(i * SUB, (i + 1) * SUB)
        cum = cum_ref[rows, :]
        tail = jnp.exp(starts[i + 1] - cum)
        high, low = halves(load_x(ref, i * SUB, SUB).astype(F32) * tail)
        b = load_b(ref, i * SUB, SUB)
        tall = jnp.concatenate([b, b], axis=0)
        states.append(dot_t(tall, jnp.concatenate([high, low], axis=0)))
        grow_ref[rows, :] = jnp.exp(cum - starts[i])
        out_ref[rows, :] = near_ref[rows, :]

    size = 1
    for bit in range(4):
        to_lanes = spread(128, 7 + bit, LEVELS)
        for group in range(1, subs // size, 2):
            rows = slice(group * size * SUB, (group + 1) * size * SUB)
            c = load_c(ref, rows.start, size * SUB)
            lower = jnp.concatenate(halves(states[group - 1]), axis=0)
            reached = dot(jnp.concatenate([c, c], axis=1), lower)
            gates = dot(gate_ref[rows, :], to_lanes)
            for part in range(size):
                i = group * size + part
                here = slice(i * SUB, (i + 1) * SUB)
                there = slice(part * SUB, (part + 1) * SUB)
                weight = gates[there] * grow_ref[here, :]
                if part:
                    weight = weight * jnp.exp(starts[i] - starts[group * size])
                out_ref[here, :] += weight * reached[there]
        states = [
            states[g] * jnp.exp(starts[(g + 2) * size] - starts[(g + 1) * size]) + states[g + 1]
            for g in range(0, subs // size, 2)
        ]
        size *= 2
    for i in range(1, subs):
        rows = slice(i * SUB, (i + 1) * SUB)
        grow_ref[rows, :] = grow_ref[rows, :] * jnp.exp(starts[i])


def levels_part(received, cum, gates, near, own):
    wide = jax.ShapeDtypeStruct((CHUNK, WIDTH), F32)
    vmem = pl.BlockSpec(memory_space=pltpu.VMEM)
    return pl.pallas_call(
        levels_kernel,
        in_specs=[vmem] * 4 + [pl.BlockSpec(memory_space=pl.ANY)],
        out_shape=(wide, wide),
        compiler_params=params(),
        cost_estimate=pl.CostEstimate(
            flops=4 * 10**9, bytes_accessed=4 * 1024 * 1024, transcendentals=10**6
        ),
        name="levels_part",
    )(received, cum, gates, near, own)


def outer_kernel(
    place_ref,
    ref,
    inner_ref,
    grow_ref,
    gate_ref,
    pair_ref,
    one_ref,
    shift_ref,
    skip_ref,
    out_ref,
):
    place = place_ref[0]
    in_half, two, three = place % 2 == 1, place // 2 == 2, place // 2 == 3
    prefix = jnp.where(in_half, message_total(pair_ref), 0.0)
    far_prefix = prefix + jnp.where(three, message_total(shift_ref), 0.0)
    shifted = message_state(shift_ref)
    levels = (
        jnp.where(in_half, message_state(pair_ref), 0.0),
        jnp.exp(prefix) * (message_state(one_ref) + jnp.where(three, shifted, 0.0)),
        jnp.exp(far_prefix) * (jnp.where(two, shifted, 0.0) + message_state(skip_ref)),
    )
    levels = [jnp.concatenate(halves(value), axis=0) for value in levels]
    spreads = [spread(128, 11 + bit, LEVELS) for bit in range(3)]
    for k in range(CHUNK // BLOCK):
        rows = slice(k * BLOCK, (k + 1) * BLOCK)
        c = load_c(ref, k * BLOCK, BLOCK)
        c = jnp.concatenate([c, c], axis=1)
        gates = gate_ref[rows, :]
        total = jnp.zeros((BLOCK, WIDTH), F32)
        for bit in range(3):
            total += dot(gates, spreads[bit]) * dot(c, levels[bit])
        mixed = inner_ref[rows, :] + grow_ref[rows, :] * total
        out_ref[k * 16 : (k + 1) * 16] = mixed.astype(BF16).reshape(BLOCK // 16, 16, WIDTH)


def outer_part(place, received, inner, grow, gates, messages):
    vmem = pl.BlockSpec(memory_space=pltpu.VMEM)
    return pl.pallas_call(
        outer_kernel,
        in_specs=[pl.BlockSpec(memory_space=pltpu.SMEM)] + [vmem] * 8,
        out_specs=vmem,
        out_shape=jax.ShapeDtypeStruct((64, 16, WIDTH), BF16),
        compiler_params=params(),
        name="outer_part",
    )(place, received, inner, grow, gates, *messages)


def unpack_kernel(ref, out_ref, held_ref, sems):
    copies = []
    for k in range(SEQS):
        for g in range(GROUPS):
            held_ref[k, :, g * WIDTH : (g + 1) * WIDTH] = ref[k * GROUPS + g]
        copy = pltpu.make_async_copy(held_ref.at[k], out_ref.at[k], sems.at[k])
        copy.start()
        copies.append(copy)
    for copy in copies:
        copy.wait()


def unpack(received):
    shape = (SEQS, 16, HEADS * HEAD_DIM)
    return pl.pallas_call(
        unpack_kernel,
        in_specs=[pl.BlockSpec(memory_space=pltpu.VMEM)],
        out_specs=pl.BlockSpec(memory_space=pltpu.HBM),
        out_shape=jax.ShapeDtypeStruct(shape, BF16),
        scratch_shapes=[pltpu.VMEM(shape, BF16), pltpu.SemaphoreType.DMA((SEQS,))],
        compiler_params=params(),
        name="unpack_outputs",
    )(received)


def per_device(x_heads, b_keys, c_queries, log_decay, level_log, skip_gain):
    near_axes = ("block", "tp")
    place = lax.axis_index("chunk").astype(jnp.int32)[None]
    packed = pack(x_heads, b_keys, c_queries, log_decay, level_log)
    received = lax.all_to_all(packed, near_axes, 0, 0, tiled=True)
    gain = jnp.repeat(skip_gain, HEAD_DIM)[None, :]
    own, cum = chunk_state(received)
    pair = lax.ppermute(own, "chunk", [(source, source ^ 1) for source in range(8)])
    near, gates = near_part(received, cum, gain)
    own = join(place, own, pair, near)

    def up(value, *steps):
        pairs = [(2 * a + half, 2 * b + 1 - half) for a, b in steps for half in (0, 1)]
        return lax.ppermute(value, "chunk", pairs)

    one = up(own, (0, 1))
    inner, grow = levels_part(received, cum, gates, near, own)
    joined, shifting = relay(place, own, one, inner)
    shift = up(shifting, (1, 2), (2, 3))
    skip = up(joined, (1, 3))
    mixed = outer_part(place, received, inner, grow, gates, [pair, one, shift, skip])
    return unpack(lax.all_to_all(mixed, near_axes, 0, 0, tiled=True))


def solution(mesh):
    cut = Mesh(mesh.devices.reshape(8, 4, 16), ("chunk", "block", "tp"))
    split = P(None, ("chunk", "block", "tp"), None)
    return jax.shard_map(
        per_device,
        mesh=cut,
        in_specs=(split, split, split, split, split, P("tp")),
        out_specs=split,
        check_vma=False,
    )
```

```python
import jax
import jax.numpy as jnp
from jax import lax
from jax.experimental import pallas as pl
from jax.experimental.pallas import tpu as pltpu
from jax.sharding import Mesh
from jax.sharding import PartitionSpec as P

SEQS = 4
HEADS = 64
HEAD_DIM = 64
STATE = 128
GROUPS = 16
PER_GROUP = 4
LEVELS = 14
NEAR_LEVELS = 9
CHUNK = 1024
BLOCK = 256
SUB = 64
ROWS = 72
WIDTH = PER_GROUP * HEAD_DIM
GATES = PER_GROUP * LEVELS
CODE = 64.0
F32 = jnp.float32
BF16 = jnp.bfloat16
VMEM_LIMIT = 48 * 1024 * 1024


def dot(a, b):
    return jnp.dot(a, b, preferred_element_type=F32)


def dot_t(a, b):
    return lax.dot_general(a, b, (((0,), (0,)), ((), ())), preferred_element_type=F32)


def dot_nt(a, b):
    return lax.dot_general(a, b, (((1,), (1,)), ((), ())), preferred_element_type=F32)


def params():
    return pltpu.CompilerParams(vmem_limit_bytes=VMEM_LIMIT)


def pack_kernel(*refs):
    sources, out_ref = refs[:5], refs[5]
    x_ref, b_ref, c_ref, decay_ref, level_ref = held = refs[6:11]
    packed_ref, sems, out_sems = refs[11:]
    copies = [
        [
            pltpu.make_async_copy(source.at[k], slot.at[k], sems.at[i, k])
            for i, (source, slot) in enumerate(zip(sources, held))
        ]
        for k in range(SEQS)
    ]
    for group in copies:
        for copy in group:
            copy.start()
    sends = []
    for k, group in enumerate(copies):
        for copy in group:
            copy.wait()
        gates = jnp.exp(CODE * level_ref[k])
        decay = decay_ref[k]
        high = decay.astype(BF16).astype(F32)
        low = decay - high
        for g in range(GROUPS):
            at = k * GROUPS + g
            packed_ref[at, 0:16, :] = x_ref[k, :, g * WIDTH : g * WIDTH + 128]
            packed_ref[at, 16:32, :] = x_ref[k, :, g * WIDTH + 128 : (g + 1) * WIDTH]
            packed_ref[at, 32:48, :] = b_ref[k, :, g * STATE : (g + 1) * STATE]
            packed_ref[at, 48:64, :] = c_ref[k, :, g * STATE : (g + 1) * STATE]
            heads = slice(g * PER_GROUP, (g + 1) * PER_GROUP)
            piece = jnp.concatenate(
                [gates[:, g * GATES : (g + 1) * GATES], high[:, heads], low[:, heads]], axis=1
            )
            packed_ref[at, 64:72, :] = jnp.concatenate([piece[0:8], piece[8:16]], axis=1).astype(BF16)
        part = pl.ds(k * GROUPS, GROUPS)
        sends.append(
            pltpu.make_async_copy(packed_ref.at[part], out_ref.at[part], out_sems.at[k])
        )
        sends[-1].start()
    for copy in sends:
        copy.wait()


def pack(*arrays):
    shape = (SEQS * GROUPS, ROWS, 128)
    return pl.pallas_call(
        pack_kernel,
        in_specs=[pl.BlockSpec(memory_space=pltpu.HBM)] * len(arrays),
        out_specs=pl.BlockSpec(memory_space=pltpu.HBM),
        out_shape=jax.ShapeDtypeStruct(shape, BF16),
        scratch_shapes=[pltpu.VMEM(a.shape, a.dtype) for a in arrays]
        + [
            pltpu.VMEM(shape, BF16),
            pltpu.SemaphoreType.DMA((len(arrays), SEQS)),
            pltpu.SemaphoreType.DMA((SEQS,)),
        ],
        name="pack_messages",
    )(*arrays)


def load_rows(ref, first, count, start, stop):
    part = ref[pl.ds(first // 16, count // 16), start:stop, :]
    return part.reshape(count, 128)


def load_x(ref, first, count):
    return jnp.concatenate(
        [load_rows(ref, first, count, 0, 16), load_rows(ref, first, count, 16, 32)], axis=1
    )


def load_b(ref, first, count):
    return load_rows(ref, first, count, 32, 48)


def load_c(ref, first, count):
    return load_rows(ref, first, count, 48, 64)


def halves_wide(value):
    high = value.astype(BF16)
    return high, value - high.astype(F32)


def halves(value):
    high = value.astype(BF16)
    return high, (value - high.astype(F32)).astype(BF16)


def spread(rows, offset, stride):
    row = lax.broadcasted_iota(jnp.int32, (rows, WIDTH), 0) % 64
    head = lax.broadcasted_iota(jnp.int32, (rows, WIDTH), 1) // HEAD_DIM
    return jnp.where(row == offset + stride * head, 1.0, 0.0).astype(BF16)


def chunk_cumsum(ref, wide_ref, cum_ref):
    both = ref[:, 64:72, :].astype(F32)
    wide_ref[:, 0:8, :] = both[:, :, 0:64]
    wide_ref[:, 8:16, :] = both[:, :, 64:128]
    row = lax.broadcasted_iota(jnp.int32, (BLOCK, BLOCK), 0)
    col = lax.broadcasted_iota(jnp.int32, (BLOCK, BLOCK), 1)
    lower = jnp.where(row >= col, 1.0, 0.0).astype(BF16)
    lane = lax.broadcasted_iota(jnp.int32, (64, WIDTH), 0)
    head = lax.broadcasted_iota(jnp.int32, (64, WIDTH), 1) // HEAD_DIM
    wanted = (lane >= GATES) & (lane % PER_GROUP == head)
    widen = jnp.where(wanted, 1.0, 0.0).astype(BF16)
    widen = jnp.concatenate([widen] * 3, axis=0)
    offset = jnp.zeros((1, WIDTH), F32)
    for k in range(CHUNK // BLOCK):
        values = wide_ref[k * 16 : (k + 1) * 16].reshape(BLOCK, 64).astype(BF16)
        sums = dot(lower, values)
        high, rest = halves_wide(sums)
        middle, rest = halves_wide(rest)
        parts = jnp.concatenate([high, middle, rest.astype(BF16)], axis=1)
        cum = dot(parts, widen) + offset
        cum_ref[k * BLOCK : (k + 1) * BLOCK, :] = cum
        offset = cum[BLOCK - 1 :, :]
    return offset


def decode_gates(ref, wide_ref, gate_ref):
    both = ref[:, 64:72, :].astype(F32)
    lane = lax.broadcasted_iota(jnp.int32, both.shape, 2) % 64
    gates = jnp.exp(jnp.log(jnp.where(lane < GATES, both, 1.0)) * (1.0 / CODE))
    wide_ref[:, 0:8, :] = gates[:, :, 0:64]
    wide_ref[:, 8:16, :] = gates[:, :, 64:128]
    high, low = halves(wide_ref[...].reshape(CHUNK, 64))
    gate_ref[...] = jnp.concatenate([high, low], axis=1)


def split_rows(total):
    high = total.astype(BF16).astype(F32)
    middle = (total - high).astype(BF16).astype(F32)
    low = total - high - middle
    row = lax.broadcasted_iota(jnp.int32, (16, WIDTH), 0)
    rows = jnp.where(row == 0, high, jnp.where(row == 1, middle, jnp.where(row == 2, low, 0.0)))
    return rows.astype(BF16)


def message_state(ref):
    return ref[0:STATE, :].astype(F32)


def message_total(ref):
    rows = ref[STATE : STATE + 16, :].astype(F32)
    return rows[0:1] + rows[1:2] + rows[2:3]


def state_kernel(ref, out_ref, cum_ref, wide_ref):
    total = chunk_cumsum(ref, wide_ref, cum_ref)
    state = jnp.zeros((STATE, WIDTH), F32)
    for k in range(CHUNK // BLOCK):
        tail = jnp.exp(total - cum_ref[k * BLOCK : (k + 1) * BLOCK, :])
        high, low = halves(load_x(ref, k * BLOCK, BLOCK).astype(F32) * tail)
        b = load_b(ref, k * BLOCK, BLOCK)
        both = dot_t(b, jnp.concatenate([high, low], axis=1))
        state += both[:, :WIDTH] + both[:, WIDTH:]
    out_ref[0:STATE, :] = state.astype(BF16)
    out_ref[STATE : STATE + 16, :] = split_rows(total)


def chunk_state(received):
    return pl.pallas_call(
        state_kernel,
        out_shape=(
            jax.ShapeDtypeStruct((STATE + 16, WIDTH), BF16),
            jax.ShapeDtypeStruct((CHUNK, WIDTH), F32),
        ),
        scratch_shapes=[pltpu.VMEM((64, 16, 64), F32)],
        compiler_params=params(),
        name="chunk_state",
    )(received)


def join_kernel(place_ref, own_ref, partner_ref, near_ref, out_ref):
    upper = place_ref[0] % 2 == 1
    own, own_total = message_state(own_ref), message_total(own_ref)
    partner, partner_total = message_state(partner_ref), message_total(partner_ref)
    late_total = jnp.where(upper, own_total, partner_total)
    early = jnp.where(upper, partner, own)
    late = jnp.where(upper, own, partner)
    out_ref[0:STATE, :] = (jnp.exp(late_total) * early + late).astype(BF16)
    out_ref[STATE : STATE + 16, :] = split_rows(own_total + partner_total)


def join(place, own, partner, near):
    return pl.pallas_call(
        join_kernel,
        in_specs=[
            pl.BlockSpec(memory_space=pltpu.SMEM),
            pl.BlockSpec(memory_space=pltpu.VMEM),
            pl.BlockSpec(memory_space=pltpu.VMEM),
            pl.BlockSpec(memory_space=pl.ANY),
        ],
        out_shape=jax.ShapeDtypeStruct(own.shape, BF16),
        compiler_params=params(),
        name="join_states",
    )(place, own, partner, near)


def relay_kernel(place_ref, own_ref, before_ref, inner_ref, out_ref, shift_ref):
    total = message_total(own_ref)
    state = jnp.exp(total) * message_state(before_ref) + message_state(own_ref)
    out_ref[0:STATE, :] = state.astype(BF16)
    out_ref[STATE : STATE + 16, :] = split_rows(total + message_total(before_ref))
    shift_ref[...] = jnp.where(place_ref[0] // 2 == 2, own_ref[...], out_ref[...])


def relay(place, own, before, inner):
    vmem = pl.BlockSpec(memory_space=pltpu.VMEM)
    message = jax.ShapeDtypeStruct(own.shape, BF16)
    return pl.pallas_call(
        relay_kernel,
        in_specs=[
            pl.BlockSpec(memory_space=pltpu.SMEM),
            vmem,
            vmem,
            pl.BlockSpec(memory_space=pl.ANY),
        ],
        out_shape=(message, message),
        compiler_params=params(),
        name="relay_states",
    )(place, own, before, inner)


def near_kernel(ref, cum_ref, gain_ref, out_ref, gate_ref, wide_ref):
    decode_gates(ref, wide_ref, gate_ref)
    gain = gain_ref[...]
    row = lax.broadcasted_iota(jnp.int32, (SUB, WIDTH), 0)
    col = lax.broadcasted_iota(jnp.int32, (SUB, WIDTH), 1) % SUB
    diagonal = row == col
    row = lax.broadcasted_iota(jnp.int32, (BLOCK, WIDTH), 0) % SUB
    col = lax.broadcasted_iota(jnp.int32, (BLOCK, WIDTH), 1) % SUB
    differ = jnp.bitwise_xor(row, col)
    causal = row >= col
    head_row = lax.broadcasted_iota(jnp.int32, (PER_GROUP * SUB, WIDTH), 0) // SUB
    head_col = lax.broadcasted_iota(jnp.int32, (PER_GROUP * SUB, WIDTH), 1) // HEAD_DIM
    same_head = head_row == head_col
    spreads = [spread(128, level, LEVELS) for level in range(7)]
    subs = BLOCK // SUB

    @pl.loop(0, CHUNK // BLOCK)
    def _(k):
        first = k * BLOCK
        cum = cum_ref[pl.ds(first, BLOCK), :]
        x = load_x(ref, first, BLOCK)
        gates = gate_ref[pl.ds(first, BLOCK), :]
        dots = dot_nt(load_c(ref, first, BLOCK), load_b(ref, first, BLOCK))
        picked = dot(gates, spreads[6])
        for level in range(5, -1, -1):
            picked = jnp.where(differ < (1 << level), dot(gates, spreads[level]), picked)
        raw, gap = [], []
        for i in range(subs):
            rows = slice(i * SUB, (i + 1) * SUB)
            raw.append(jnp.concatenate([dots[rows, rows]] * PER_GROUP, axis=1))
            cum_row = jnp.sum(jnp.where(diagonal, cum[rows], 0.0), axis=0, keepdims=True)
            gap.append(cum[rows] - cum_row)
        decay = jnp.exp(jnp.minimum(jnp.concatenate(gap, axis=0), 0.0))
        raw = jnp.concatenate(raw, axis=0)
        scores = jnp.where(causal, raw * decay * picked, 0.0).astype(BF16)
        skip = gain * x.astype(F32)
        for i in range(subs):
            rows = slice(i * SUB, (i + 1) * SUB)
            tall_x = jnp.concatenate([x[rows]] * PER_GROUP, axis=0)
            block_x = jnp.where(same_head, tall_x, jnp.zeros_like(tall_x))
            out_ref[pl.ds(first + i * SUB, SUB), :] = dot(scores[rows], block_x) + skip[rows]


def near_part(received, cum, gain):
    return pl.pallas_call(
        near_kernel,
        out_shape=(
            jax.ShapeDtypeStruct((CHUNK, WIDTH), F32),
            jax.ShapeDtypeStruct((CHUNK, 128), BF16),
        ),
        scratch_shapes=[pltpu.VMEM((64, 16, 64), F32)],
        compiler_params=params(),
        cost_estimate=pl.CostEstimate(
            flops=4 * 10**9, bytes_accessed=4 * 1024 * 1024, transcendentals=10**6
        ),
        name="near_part",
    )(received, cum, gain)


def levels_kernel(
    place_ref, ref, cum_ref, gate_ref, near_ref, pair_ref, own_ref, out_ref, grow_ref
):
    subs = CHUNK // SUB
    starts = [jnp.zeros((1, WIDTH), F32)]
    starts += [cum_ref[i * SUB - 1 : i * SUB, :] for i in range(1, subs + 1)]
    states = []
    for i in range(subs):
        rows = slice(i * SUB, (i + 1) * SUB)
        cum = cum_ref[rows, :]
        tail = jnp.exp(starts[i + 1] - cum)
        high, low = halves(load_x(ref, i * SUB, SUB).astype(F32) * tail)
        b = load_b(ref, i * SUB, SUB)
        tall = jnp.concatenate([b, b], axis=0)
        states.append(dot_t(tall, jnp.concatenate([high, low], axis=0)))
        grow_ref[rows, :] = jnp.exp(cum - starts[i])
        out_ref[rows, :] = near_ref[rows, :]

    size = 1
    for bit in range(4):
        to_lanes = spread(128, 7 + bit, LEVELS)
        for group in range(1, subs // size, 2):
            rows = slice(group * size * SUB, (group + 1) * size * SUB)
            c = load_c(ref, rows.start, size * SUB)
            lower = jnp.concatenate(halves(states[group - 1]), axis=0)
            reached = dot(jnp.concatenate([c, c], axis=1), lower)
            gates = dot(gate_ref[rows, :], to_lanes)
            for part in range(size):
                i = group * size + part
                here = slice(i * SUB, (i + 1) * SUB)
                there = slice(part * SUB, (part + 1) * SUB)
                weight = gates[there] * grow_ref[here, :]
                if part:
                    weight = weight * jnp.exp(starts[i] - starts[group * size])
                out_ref[here, :] += weight * reached[there]
        states = [
            states[g] * jnp.exp(starts[(g + 2) * size] - starts[(g + 1) * size]) + states[g + 1]
            for g in range(0, subs // size, 2)
        ]
        size *= 2
    for i in range(1, subs):
        rows = slice(i * SUB, (i + 1) * SUB)
        grow_ref[rows, :] = grow_ref[rows, :] * jnp.exp(starts[i])
    other = jnp.where(place_ref[0] % 2 == 1, message_state(pair_ref), 0.0)
    other = jnp.concatenate(halves(other), axis=0)
    to_lanes = spread(128, 11, LEVELS)
    for k in range(CHUNK // BLOCK):
        rows = slice(k * BLOCK, (k + 1) * BLOCK)
        c = load_c(ref, k * BLOCK, BLOCK)
        reached = dot(jnp.concatenate([c, c], axis=1), other)
        out_ref[rows, :] += dot(gate_ref[rows, :], to_lanes) * grow_ref[rows, :] * reached


def levels_part(place, received, cum, gates, near, pair, own):
    wide = jax.ShapeDtypeStruct((CHUNK, WIDTH), F32)
    vmem = pl.BlockSpec(memory_space=pltpu.VMEM)
    return pl.pallas_call(
        levels_kernel,
        in_specs=[pl.BlockSpec(memory_space=pltpu.SMEM)]
        + [vmem] * 5
        + [pl.BlockSpec(memory_space=pl.ANY)],
        out_shape=(wide, wide),
        compiler_params=params(),
        cost_estimate=pl.CostEstimate(
            flops=4 * 10**9, bytes_accessed=4 * 1024 * 1024, transcendentals=10**6
        ),
        name="levels_part",
    )(place, received, cum, gates, near, pair, own)


def outer_kernel(
    place_ref,
    ref,
    inner_ref,
    grow_ref,
    gate_ref,
    pair_ref,
    one_ref,
    shift_ref,
    skip_ref,
    out_ref,
):
    place = place_ref[0]
    in_half, two, three = place % 2 == 1, place // 2 == 2, place // 2 == 3
    prefix = jnp.where(in_half, message_total(pair_ref), 0.0)
    far_prefix = prefix + jnp.where(three, message_total(shift_ref), 0.0)
    shifted = message_state(shift_ref)
    levels = (
        jnp.exp(prefix) * (message_state(one_ref) + jnp.where(three, shifted, 0.0)),
        jnp.exp(far_prefix) * (jnp.where(two, shifted, 0.0) + message_state(skip_ref)),
    )
    levels = [jnp.concatenate(halves(value), axis=0) for value in levels]
    spreads = [spread(128, 12 + bit, LEVELS) for bit in range(2)]
    for k in range(CHUNK // BLOCK):
        rows = slice(k * BLOCK, (k + 1) * BLOCK)
        c = load_c(ref, k * BLOCK, BLOCK)
        c = jnp.concatenate([c, c], axis=1)
        gates = gate_ref[rows, :]
        total = jnp.zeros((BLOCK, WIDTH), F32)
        for bit in range(2):
            total += dot(gates, spreads[bit]) * dot(c, levels[bit])
        mixed = inner_ref[rows, :] + grow_ref[rows, :] * total
        out_ref[k * 16 : (k + 1) * 16] = mixed.astype(BF16).reshape(BLOCK // 16, 16, WIDTH)


def outer_part(place, received, inner, grow, gates, messages):
    vmem = pl.BlockSpec(memory_space=pltpu.VMEM)
    return pl.pallas_call(
        outer_kernel,
        in_specs=[pl.BlockSpec(memory_space=pltpu.SMEM)] + [vmem] * 8,
        out_specs=vmem,
        out_shape=jax.ShapeDtypeStruct((64, 16, WIDTH), BF16),
        compiler_params=params(),
        name="outer_part",
    )(place, received, inner, grow, gates, *messages)


def unpack_kernel(ref, out_ref, held_ref, sems):
    copies = []
    for k in range(SEQS):
        for g in range(GROUPS):
            held_ref[k, :, g * WIDTH : (g + 1) * WIDTH] = ref[k * GROUPS + g]
        copy = pltpu.make_async_copy(held_ref.at[k], out_ref.at[k], sems.at[k])
        copy.start()
        copies.append(copy)
    for copy in copies:
        copy.wait()


def unpack(received):
    shape = (SEQS, 16, HEADS * HEAD_DIM)
    return pl.pallas_call(
        unpack_kernel,
        in_specs=[pl.BlockSpec(memory_space=pltpu.VMEM)],
        out_specs=pl.BlockSpec(memory_space=pltpu.HBM),
        out_shape=jax.ShapeDtypeStruct(shape, BF16),
        scratch_shapes=[pltpu.VMEM(shape, BF16), pltpu.SemaphoreType.DMA((SEQS,))],
        compiler_params=params(),
        name="unpack_outputs",
    )(received)


def per_device(x_heads, b_keys, c_queries, log_decay, level_log, skip_gain):
    near_axes = ("block", "tp")
    place = lax.axis_index("chunk").astype(jnp.int32)[None]
    packed = pack(x_heads, b_keys, c_queries, log_decay, level_log)
    received = lax.all_to_all(packed, near_axes, 0, 0, tiled=True)
    gain = jnp.repeat(skip_gain, HEAD_DIM)[None, :]
    own, cum = chunk_state(received)
    pair = lax.ppermute(own, "chunk", [(source, source ^ 1) for source in range(8)])
    near, gates = near_part(received, cum, gain)
    own = join(place, own, pair, near)

    def up(value, *steps):
        pairs = [(2 * a + half, 2 * b + 1 - half) for a, b in steps for half in (0, 1)]
        return lax.ppermute(value, "chunk", pairs)

    one = up(own, (0, 1))
    inner, grow = levels_part(place, received, cum, gates, near, pair, own)
    joined, shifting = relay(place, own, one, inner)
    shift = up(shifting, (1, 2), (2, 3))
    skip = up(joined, (1, 3))
    mixed = outer_part(place, received, inner, grow, gates, [pair, one, shift, skip])
    return unpack(lax.all_to_all(mixed, near_axes, 0, 0, tiled=True))


def solution(mesh):
    cut = Mesh(mesh.devices.reshape(8, 4, 16), ("chunk", "block", "tp"))
    split = P(None, ("chunk", "block", "tp"), None)
    return jax.shard_map(
        per_device,
        mesh=cut,
        in_specs=(split, split, split, split, split, P("tp")),
        out_specs=split,
        check_vma=False,
    )
```
